128 devices in a mesh: sec: 2 (over core), dev: 64 (over z, x, y).
Axes of the slice: x: 4, y: 4, z: 4, core: 2. Of those that a mesh axis runs over, the one named last changes fastest.
Arguments:
- hidden_state: bfloat16 [4096, 2048], P(('sec', 'dev')), may hold values from -6 to 6
- queries: bfloat16 [4096, 2048], P(('sec', 'dev')), may hold values from -7 to 7
- new_keys: bfloat16 [4096, 256], P(('sec', 'dev')), may hold values from -4 to 4
- new_values: bfloat16 [4096, 256], P(('sec', 'dev')), may hold values from -6 to 6
- cache_keys: bfloat16 [4096, 96, 256], P(('sec', 'dev')), may hold values from -7 to 7
- cache_values: bfloat16 [4096, 96, 256], P(('sec', 'dev')), may hold values from -6 to 6
- lengths: int32 [4096], P(('sec', 'dev')), may hold values from 2 to 96, as said below
- o_weight: bfloat16 [2048, 2048], replicated, may hold values from -0.125 to 0.125
- norm_gain: float32 [2048], replicated, may hold values from 0.1 to 1.9
- expert_ids: int32 [4096, 8], P(('sec', 'dev')), may hold values from 0 to 127, all different within a row; in each aligned block of 16 rows (0 to 15, 16 to 31, ...) at most 2 rows name the same one
- gate_values: float32 [4096, 8], P(('sec', 'dev')), may hold values from 0.05 to 1
- w_gate: bfloat16 [128, 2048, 768], P(('sec', 'dev')), may hold values from -0.125 to 0.125
- w_up: bfloat16 [128, 2048, 768], P(('sec', 'dev')), may hold values from -0.125 to 0.125
- w_down: bfloat16 [128, 768, 2048], P(('sec', 'dev')), may hold values from -0.21875 to 0.21875
Outputs:
- new_hidden: bfloat16 [4096, 2048], P(('sec', 'dev'))
The draws below stay inside these ranges and needn't reach their ends.
Inputs may be any that keep to these rules, and one draw needn't show every extreme that they name: `lengths`: every row has at least 2 live positions, and some row has 96. `expert_ids`: within each aligned block of 16 rows (one micro-batch of one device) no expert is named by more than 2 rows; in some blocks one expert is named by exactly 2.
All inputs are finite; a program needn't handle non-finite values.
Results may differ from the reference program's by a relative error of at most 0.02.
Values may be sent and summed in bfloat16 or wider, within the bound.
No kernel may reach another device: no remote copies, remote signals or barrier semaphores. Data moves between devices by JAX's collectives and lax.ppermute only.
A program may use at most 128 MiB of HBM per device.

```python
import math
import jax
import jax.numpy as jnp
import numpy as np
from jax import lax

D = 2048
FF = 768
HEADS = 16
KV_HEADS = 2
HEAD_DIM = 128
GROUP = 8
TOP = 8
EXPERTS = 128
MICRO = 16
ROWS_DEV = 32
ROWS = 4096
LMAX = 96
MOST = 2
N_SEC = 2
N_DEV = 64


def draw_queries(key, part):
    key = jax.random.fold_in(key, 11)
    base_draw = jax.random.truncated_normal(key, -4.0, 4.0, (ROWS, HEADS, HEAD_DIM), jnp.float32)
    return base_draw.reshape(ROWS, HEADS * HEAD_DIM).astype(jnp.bfloat16)


def draw_cache_keys(key, part):
    key = jax.random.fold_in(key, 12)
    base_draw = jax.random.truncated_normal(key, -4.0, 4.0, (ROWS, LMAX, KV_HEADS, HEAD_DIM), jnp.float32)
    return base_draw.reshape(ROWS, LMAX, KV_HEADS * HEAD_DIM).astype(jnp.bfloat16)


def draw_lengths(key, part):
    key = jax.random.fold_in(key, 13)
    key_shift, key_raw, key_peak = jax.random.split(key, 3)
    shift_bits = jax.random.randint(key_shift, (ROWS // ROWS_DEV,), 0, 3)
    raw_lengths = jax.random.randint(key_raw, (ROWS,), 2, LMAX + 1)
    row_lengths = jnp.maximum(raw_lengths >> jnp.repeat(shift_bits, ROWS_DEV), 2)
    peak_row = jax.random.randint(key_peak, (), 0, ROWS)
    return jnp.where(jnp.arange(ROWS) == peak_row, LMAX, row_lengths).astype(jnp.int32)


def block_levels(stream_key, shape, cuts, least, top_value):
    gain = 1.0
    for dim, shards_of in cuts:
        steps = jax.random.uniform(jax.random.fold_in(jax.random.fold_in(stream_key, 6), dim), (shards_of,), jnp.float32, least / len(cuts), top_value / len(cuts))
        gain = gain * jnp.repeat(jnp.exp(steps), shape[dim] // shards_of).reshape((-1,) + (1,) * (len(shape) - 1 - dim))
    return gain


def shared_out(key, own, number, rows, count, top, bound, slope):
    order = jax.random.permutation(key, count)
    heavy_load, usual = load_shares(count, rows * top, bound, slope, True), load_shares(count, rows * top, bound, slope, False)
    places = jnp.arange(count)

    def named(tallies, offset_by):
        used = int((tallies > 0).sum())
        fixed = max(1, used // 4)
        passed = fixed + (places - fixed + offset_by * (used - fixed)) % max(1, count - fixed)
        return jnp.zeros((count,), jnp.int32).at[order[jnp.where(places < fixed, places, passed)]].set(jnp.asarray(tallies, jnp.int32))

    tallies = jnp.where(number % 4 == 0, named(heavy_load, number // 4), named(usual, number - number // 4 - 1))
    mixed = jax.random.permutation(jax.random.fold_in(own, 3), count)
    donor, receiver = mixed[0:count // 2 * 2:2], mixed[1:count // 2 * 2:2]
    margin = jnp.minimum(tallies[donor] - 1, bound - tallies[receiver]) // 2
    margin = jnp.where((donor == order[0]) | (receiver == order[0]) | (tallies[receiver] == 0), 0, jnp.maximum(margin, 0))
    passed = jax.random.randint(jax.random.fold_in(own, 4), (count // 2,), 0, 1 << 20) % (margin + 1)
    tallies = tallies.at[donor].add(-passed).at[receiver].add(passed)
    items = jnp.searchsorted(jnp.cumsum(tallies), jnp.arange(rows * top), side="right").astype(jnp.int32)
    listing = items.reshape(top, rows).T
    listing = listing[jax.random.permutation(jax.random.fold_in(own, 1), rows)]
    offset_by = jax.random.randint(jax.random.fold_in(own, 2), (rows, 1), 0, top)
    return jnp.take_along_axis(listing, (jnp.arange(top)[None, :] + offset_by) % top, axis=1)


def load_shares(amount, total, most, skew, full):
    loads = [(1 << 20) // math.isqrt(standing ** skew) + 1 for standing in range(1, amount + 1)]
    largest = most if full else min(most, max(-(-total // amount), total * loads[0] // sum(loads)))
    least = 1 if total - largest >= amount - 1 else 0
    given, surplus = [largest] + [least] * (amount - 1), total - largest - least * (amount - 1)
    while surplus > 0:
        movable = [i for i in range(1, amount) if given[i] < largest] or [i for i in range(1, amount) if given[i] < most]
        pool, left = sum([loads[i] for i in movable]), surplus
        for i in movable:
            more = min(most - given[i], max(1, left * loads[i] // pool), surplus)
            given[i] = given[i] + more
            surplus = surplus - more
    return np.array(given)


def gaussian(stream_key, shape, width, limit, shards=(), held_as=jnp.bfloat16):
    values = width * jax.random.normal(stream_key, shape, jnp.float32)
    if shards:
        values = values * block_levels(stream_key, shape, shards, -0.22, 0.18)
    return jnp.clip(values, -limit, limit).astype(held_as)


def setup_inputs(seed: int = 0) -> dict:
    key_of = jax.random.split(jax.random.key(seed), 15)
    hidden_state = gaussian(key_of[0], (ROWS, D), 1.0, 6.0, ((0, 128),))
    queries = draw_queries(jax.random.fold_in(key_of[14], 71), 0)
    new_keys = gaussian(key_of[2], (ROWS, KV_HEADS * HEAD_DIM), 1.0, 4.0, ((0, 128),))
    new_values = gaussian(key_of[3], (ROWS, KV_HEADS * HEAD_DIM), 1.0, 6.0, ((0, 128),))
    cache_keys = draw_cache_keys(jax.random.fold_in(key_of[14], 71), 0)
    cache_values = gaussian(key_of[5], (ROWS, LMAX, KV_HEADS * HEAD_DIM), 1.0, 6.0, ((0, 128),))
    lengths = draw_lengths(jax.random.fold_in(key_of[14], 71), 0)
    o_weight = gaussian(key_of[7], (HEADS * HEAD_DIM, D), (HEADS * HEAD_DIM) ** -0.5, 0.125)
    norm_gain = jnp.clip(1.0 + 0.18 * jax.random.normal(key_of[8], (D,), jnp.float32), 0.1, 1.9)
    expert_ids_keys = jax.random.split(jax.random.fold_in(key_of[9], 1), ROWS // MICRO)
    expert_ids_turns = jax.random.permutation(jax.random.fold_in(key_of[9], 3), ROWS // MICRO)
    expert_ids = jax.vmap(lambda own, number: shared_out(jax.random.fold_in(key_of[9], 2), own, number, MICRO, EXPERTS, TOP, MOST, 2))(expert_ids_keys, expert_ids_turns).reshape((ROWS, TOP))
    gate_values = jnp.clip(jnp.exp(math.log(1.0) - 2.9957323 * jax.random.uniform(key_of[10], (ROWS, TOP), jnp.float32) ** block_levels(key_of[10], (ROWS, TOP), ((0, 128),), -0.2, 0.2)), 0.05, 1.0)
    w_gate = gaussian(key_of[11], (EXPERTS, D, FF), D ** -0.5, 0.125, ((0, 128),))
    w_up = gaussian(key_of[12], (EXPERTS, D, FF), D ** -0.5, 0.125, ((0, 128),))
    w_down = gaussian(key_of[13], (EXPERTS, FF, D), FF ** -0.5, 0.21875, ((0, 128),))
    return dict(hidden_state=hidden_state, queries=queries, new_keys=new_keys, new_values=new_values, cache_keys=cache_keys, cache_values=cache_values, lengths=lengths, o_weight=o_weight, norm_gain=norm_gain, expert_ids=expert_ids, gate_values=gate_values, w_gate=w_gate, w_up=w_up, w_down=w_down)


def attend(query_rows, new_key_rows, new_value_rows, key_rows, value_rows, length_rows):
    row_count = query_rows.shape[0]
    score_scale = HEAD_DIM ** (-0.5)
    query_heads = query_rows.astype(jnp.float32).reshape(row_count, KV_HEADS, GROUP, HEAD_DIM)
    key_heads = key_rows.astype(jnp.float32).reshape(row_count, LMAX, KV_HEADS, HEAD_DIM)
    value_heads = value_rows.astype(jnp.float32).reshape(row_count, LMAX, KV_HEADS, HEAD_DIM)
    scores = jnp.einsum('rkgd,rlkd->rkgl', query_heads, key_heads) * score_scale
    live_mask = jnp.arange(LMAX, dtype=jnp.int32)[None, :] < length_rows[:, None]
    scores = jnp.where(live_mask[:, None, None, :], scores, -jnp.inf)
    own_key = new_key_rows.astype(jnp.float32).reshape(row_count, KV_HEADS, HEAD_DIM)
    own_score = jnp.einsum('rkgd,rkd->rkg', query_heads, own_key) * score_scale
    peak = jnp.maximum(lax.optimization_barrier(jnp.max(scores, axis=-1)), own_score)
    weights_raw = jnp.exp(scores - peak[..., None])
    weight_own = jnp.exp(own_score - peak)
    denominator = lax.optimization_barrier(jnp.sum(weights_raw, axis=-1)) + weight_own
    attn_probs = (weights_raw / denominator[..., None]).astype(jnp.bfloat16)
    probs_own = (weight_own / denominator).astype(jnp.bfloat16)
    own_value = new_value_rows.astype(jnp.float32).reshape(row_count, KV_HEADS, 1, HEAD_DIM)
    attn_out = jnp.einsum('rkgl,rlkd->rkgd', attn_probs.astype(jnp.float32), value_heads)
    attn_out = attn_out + probs_own.astype(jnp.float32)[..., None] * own_value
    return attn_out.reshape(row_count, HEADS * HEAD_DIM).astype(jnp.bfloat16)

def reference(hidden_state, queries, new_keys, new_values, cache_keys, cache_values, lengths, o_weight, norm_gain, expert_ids, gate_values, w_gate, w_up, w_down):
    blocks = ROWS // ROWS_DEV

    def blockwise(array):
        return array.reshape((blocks, ROWS_DEV) + array.shape[1:])

    def attend_block(pieces):
        return attend(*pieces)
    attended = lax.map(attend_block, (blockwise(queries), blockwise(new_keys), blockwise(new_values), blockwise(cache_keys), blockwise(cache_values), blockwise(lengths)))
    attended = attended.reshape(ROWS, HEADS * HEAD_DIM)
    after_attn = (hidden_state.astype(jnp.float32) + jnp.dot(attended, o_weight, preferred_element_type=jnp.float32)).astype(jnp.bfloat16)
    after_float = after_attn.astype(jnp.float32)
    normed = (after_float * lax.rsqrt(lax.optimization_barrier(jnp.mean(after_float * after_float, axis=-1, keepdims=True)) + 1e-06) * norm_gain).astype(jnp.bfloat16)
    count_all = ROWS * TOP
    capacity = 2 * MOST * N_SEC * N_DEV
    flat_ids = expert_ids.reshape(-1)
    sort_order = jnp.argsort(flat_ids, stable=True).astype(jnp.int32)
    counts = jnp.zeros((EXPERTS,), jnp.int32).at[flat_ids].add(1)
    starts = jnp.cumsum(counts) - counts
    slot_range = jnp.arange(capacity, dtype=jnp.int32)

    def one_expert(expert_index):
        slot_pick = jnp.minimum(starts[expert_index] + slot_range, count_all - 1)
        valid_mask = slot_range < counts[expert_index]
        pick_rows = sort_order[slot_pick]
        expert_rows = normed[pick_rows // TOP]
        gate_part = jnp.dot(expert_rows, w_gate[expert_index], preferred_element_type=jnp.float32)
        up_part = jnp.dot(expert_rows, w_up[expert_index], preferred_element_type=jnp.float32)
        hidden_act = (jax.nn.silu(gate_part) * up_part).astype(jnp.bfloat16)
        out_rows = jnp.dot(hidden_act, w_down[expert_index], preferred_element_type=jnp.float32).astype(jnp.bfloat16)
        return (out_rows, pick_rows, valid_mask)
    expert_outs, picks, valids = lax.map(one_expert, jnp.arange(EXPERTS, dtype=jnp.int32))
    targets = jnp.where(valids, picks, count_all).reshape(-1)
    gathered = jnp.zeros((count_all, D), jnp.float32).at[targets].add(expert_outs.reshape(-1, D).astype(jnp.float32), mode='drop')
    picked = gathered.reshape(ROWS, TOP, D)
    mixture = lax.optimization_barrier(jnp.sum(picked * gate_values[:, :, None], axis=1))
    return (after_float + mixture).astype(jnp.bfloat16)
```

```python
import jax
import jax.numpy as jnp
from jax import lax
from jax.experimental import pallas as pl
from jax.experimental.pallas import tpu as pltpu
from jax.sharding import PartitionSpec as P

D = 2048
FF = 768
KV_HEADS = 2
HEAD_DIM = 128
GROUP = 8
TOP = 8
MICRO = 16
ROWS_DEV = 32
LMAX = 96
MOST = 2
EXPERTS = 128

SLOTS = MOST * ROWS_DEV // MICRO
CHUNK_ROWS = 16
CHUNK_COLS = SLOTS * D // CHUNK_ROWS
BLOCKS = CHUNK_ROWS // SLOTS
LINES = EXPERTS * CHUNK_ROWS
TALL = BLOCKS * ROWS_DEV

SUB = 8
GROUPS = ROWS_DEV // SUB
O_CHUNKS = 8
O_DEPTH = D // O_CHUNKS
O_STARTS = O_CHUNKS // GROUPS
WEIGHT_PARTS = 4
W_STARTS = 2
FF_CHUNK = 256

SHUFFLE = 256
SOURCES = SHUFFLE // CHUNK_ROWS
BAND = SOURCES * SLOTS
SHUFFLES = LINES // SHUFFLE

MIB = 2**20
F32 = jnp.float32
BF16 = jnp.bfloat16
NT = (((1,), (1,)), ((), ()))
VMEM = pl.BlockSpec(memory_space=pltpu.VMEM)
SMEM = pl.BlockSpec(memory_space=pltpu.SMEM)
HBM = pl.BlockSpec(memory_space=pltpu.HBM)


def iota(shape, dim):
    return lax.broadcasted_iota(jnp.int32, shape, dim)


def dot(a, b):
    return jnp.dot(a, b, preferred_element_type=F32)


def tile_lanes(array):
    return jnp.concatenate([array] * BLOCKS, axis=1)


def slot_table(ids):
    ids = tile_lanes(ids)
    expert = iota((EXPERTS, TALL), 0)
    named = jnp.zeros((EXPERTS, TALL), F32)
    for k in range(TOP):
        named = jnp.where(ids[k : k + 1, :] == expert, 1.0, named)
    first, second = iota((TALL, TALL), 0), iota((TALL, TALL), 1)
    before = jnp.where((first // MICRO == second // MICRO) & (first < second), 1.0, 0.0)
    earlier = dot(named.astype(BF16), before.astype(BF16))
    micro = (iota((EXPERTS, TALL), 1) % ROWS_DEV) // MICRO
    return named * (earlier + (micro * MOST + 1).astype(F32))


def attend_group(group, lengths_ref, queries, new_keys, new_values, keys, values, attended):
    scale = HEAD_DIM ** (-0.5)
    mine = pl.ds(group * SUB, SUB)
    query = queries[mine, :].astype(F32)
    own_key = new_keys[mine, :].astype(F32)
    own_value = new_values[mine, :].astype(F32)
    cache = pl.ds(group * SUB * LMAX, SUB * LMAX)
    row = iota((SUB, SUB * LMAX), 0)
    length = jnp.zeros((SUB, SUB * LMAX), jnp.int32)
    for r in range(SUB):
        length = jnp.where(row == r, lengths_ref[group * SUB + r], length)
    place = iota((SUB, SUB * LMAX), 1) - row * LMAX
    bias = jnp.where((place >= 0) & (place < length), 0.0, -jnp.inf)
    bias = jnp.concatenate([bias] * GROUP, axis=0)
    for kv in range(KV_HEADS):
        cols = slice(kv * HEAD_DIM, (kv + 1) * HEAD_DIM)
        first = kv * GROUP * HEAD_DIM
        heads = jnp.concatenate(
            [query[:, first + g * HEAD_DIM : first + (g + 1) * HEAD_DIM] for g in range(GROUP)],
            axis=0,
        )
        key_tall = jnp.concatenate([own_key[:, cols]] * GROUP, axis=0)
        value_tall = jnp.concatenate([own_value[:, cols]] * GROUP, axis=0)
        scores = lax.dot_general(
            heads.astype(BF16), keys[cache, cols], NT, preferred_element_type=F32
        )
        scores = scores * scale + bias
        own = jnp.sum(heads * key_tall, axis=1, keepdims=True) * scale
        peak = jnp.maximum(jnp.max(scores, axis=1, keepdims=True), own)
        raw = jnp.exp(scores - peak)
        raw_own = jnp.exp(own - peak)
        share = 1.0 / (jnp.sum(raw, axis=1, keepdims=True) + raw_own)
        probs = (raw * share).astype(BF16)
        probs_own = (raw_own * share).astype(BF16).astype(F32)
        result = dot(probs, values[cache, cols]) + probs_own * value_tall
        for g in range(GROUP):
            attended[mine, first + g * HEAD_DIM : first + (g + 1) * HEAD_DIM] = result[
                g * SUB : (g + 1) * SUB, :
            ]


def combine_weights(table, ids, gates):
    ids = tile_lanes(ids)
    gates = tile_lanes(gates)
    expert = iota((EXPERTS, TALL), 0)
    gate = jnp.zeros((EXPERTS, TALL), F32)
    for k in range(TOP):
        gate = jnp.where(ids[k : k + 1, :] == expert, gates[k : k + 1, :], gate)
    gate = jnp.transpose(gate)
    high = gate.astype(BF16)
    low = (gate - high.astype(F32)).astype(BF16)
    table = jnp.transpose(table).astype(BF16)
    lane = iota((EXPERTS, LINES), 1)
    spread = (lane // CHUNK_ROWS == iota((EXPERTS, LINES), 0)).astype(BF16)
    lane = iota((TALL, LINES), 1)
    wanted = jnp.where(
        (lane // SLOTS) % BLOCKS == iota((TALL, LINES), 0) // ROWS_DEV,
        (lane % SLOTS + 1).astype(F32),
        -1.0,
    )
    live = dot(table, spread) == wanted
    return [jnp.where(live, dot(part, spread), 0.0).astype(BF16) for part in (high, low)]


def dispatch_weights(table):
    line = iota((LINES, EXPERTS), 0)
    spread = (line // CHUNK_ROWS == iota((LINES, EXPERTS), 1)).astype(BF16)
    wanted = jnp.where(
        (line // SLOTS) % BLOCKS == iota((LINES, TALL), 1) // ROWS_DEV,
        (line % SLOTS + 1).astype(F32),
        -1.0,
    )
    return jnp.where(dot(spread, table.astype(BF16)) == wanted, 1.0, 0.0).astype(BF16)


def attention_kernel(
    lengths_ref,
    ids_ref,
    gates_ref,
    gain_ref,
    hidden_hbm,
    queries_hbm,
    new_keys_hbm,
    new_values_hbm,
    keys_hbm,
    values_hbm,
    o_hbm,
    gate_hbm,
    up_hbm,
    down_hbm,
    after_ref,
    outgoing_ref,
    mixing_ref,
    gate_ref,
    up_ref,
    down_ref,
    hidden,
    queries,
    new_keys,
    new_values,
    keys,
    values,
    o_weight,
    attended,
    dispatch,
    small_sem,
    key_sem,
    value_sem,
    o_sem,
    weight_sem,
):
    small = [
        pltpu.make_async_copy(queries_hbm, queries, small_sem.at[0]),
        pltpu.make_async_copy(new_keys_hbm, new_keys, small_sem.at[1]),
        pltpu.make_async_copy(new_values_hbm, new_values, small_sem.at[2]),
        pltpu.make_async_copy(hidden_hbm, hidden, small_sem.at[3]),
    ]
    for copy in small:
        copy.start()
    key_copies, value_copies, o_copies = [], [], []
    for group in range(GROUPS):
        part = pl.ds(group * SUB * LMAX, SUB * LMAX)
        key_copies.append(
            pltpu.make_async_copy(keys_hbm.at[part], keys.at[part], key_sem.at[group])
        )
        value_copies.append(
            pltpu.make_async_copy(values_hbm.at[part], values.at[part], value_sem.at[group])
        )
        key_copies[group].start()
        value_copies[group].start()
    for c in range(O_CHUNKS):
        part = pl.ds(c * O_DEPTH, O_DEPTH)
        o_copies.append(pltpu.make_async_copy(o_hbm.at[part], o_weight.at[part], o_sem.at[c]))
    weight_copies = []
    for i, (source, target) in enumerate(
        ((gate_hbm, gate_ref), (up_hbm, up_ref), (down_hbm, down_ref))
    ):
        depth = source.shape[0] // WEIGHT_PARTS
        for c in range(WEIGHT_PARTS):
            part = pl.ds(c * depth, depth)
            weight_copies.append(
                pltpu.make_async_copy(source.at[part], target.at[part], weight_sem.at[i, c])
            )

    table = slot_table(ids_ref[...])
    dispatch[...] = dispatch_weights(table)
    high, low = combine_weights(table, ids_ref[...], gates_ref[...])
    mixing_ref[:TALL, :] = high
    mixing_ref[TALL:, :] = low

    for copy in small:
        copy.wait()
    waiting = list(o_copies)
    for group in range(GROUPS):
        key_copies[group].wait()
        value_copies[group].wait()
        for copy in waiting[:O_STARTS]:
            copy.start()
        waiting = waiting[O_STARTS:]
        attend_group(group, lengths_ref, queries, new_keys, new_values, keys, values, attended)

    total = hidden[...].astype(F32)
    waiting = list(weight_copies)
    for c in range(O_CHUNKS):
        o_copies[c].wait()
        for copy in waiting[:W_STARTS]:
            copy.start()
        waiting = waiting[W_STARTS:]
        part = slice(c * O_DEPTH, (c + 1) * O_DEPTH)
        total = total + dot(attended[:, part].astype(BF16), o_weight[part, :])
    after = total.astype(BF16)
    after_ref[...] = after
    after = after.astype(F32)
    mean = jnp.mean(after * after, axis=1, keepdims=True)
    normed = (after * lax.rsqrt(mean + 1e-6) * gain_ref[...]).astype(BF16)
    stacked = jnp.concatenate(
        [normed[:, q * CHUNK_COLS : (q + 1) * CHUNK_COLS] for q in range(BLOCKS)], axis=0
    )
    outgoing_ref[...] = dot(dispatch[...], stacked).astype(BF16)
    for copy in weight_copies:
        copy.wait()


def attention_part(
    lengths,
    ids,
    gates,
    gain,
    hidden,
    queries,
    new_keys,
    new_values,
    keys,
    values,
    o_weight,
    w_gate,
    w_up,
    w_down,
):
    cache = (ROWS_DEV * LMAX, KV_HEADS * HEAD_DIM)
    return pl.pallas_call(
        attention_kernel,
        out_shape=(
            pltpu.VMEM((ROWS_DEV, D), BF16),
            pltpu.VMEM((LINES, CHUNK_COLS), BF16),
            pltpu.VMEM((2 * TALL, LINES), BF16),
            pltpu.VMEM((D, FF), BF16),
            pltpu.VMEM((D, FF), BF16),
            pltpu.VMEM((FF, D), BF16),
        ),
        in_specs=[SMEM] + [VMEM] * 3 + [HBM] * 10,
        out_specs=(VMEM,) * 6,
        scratch_shapes=[
            pltpu.VMEM((ROWS_DEV, D), BF16),
            pltpu.VMEM((ROWS_DEV, D), BF16),
            pltpu.VMEM((ROWS_DEV, KV_HEADS * HEAD_DIM), BF16),
            pltpu.VMEM((ROWS_DEV, KV_HEADS * HEAD_DIM), BF16),
            pltpu.VMEM(cache, BF16),
            pltpu.VMEM(cache, BF16),
            pltpu.VMEM((D, D), BF16),
            pltpu.VMEM((ROWS_DEV, D), F32),
            pltpu.VMEM((LINES, TALL), BF16),
            pltpu.SemaphoreType.DMA((4,)),
            pltpu.SemaphoreType.DMA((GROUPS,)),
            pltpu.SemaphoreType.DMA((GROUPS,)),
            pltpu.SemaphoreType.DMA((O_CHUNKS,)),
            pltpu.SemaphoreType.DMA((3, WEIGHT_PARTS)),
        ],
        compiler_params=pltpu.CompilerParams(vmem_limit_bytes=50 * MIB),
        cost_estimate=pl.CostEstimate(
            flops=2 * ROWS_DEV * D * D, bytes_accessed=16 * MIB, transcendentals=0
        ),
        name="attend",
    )(
        lengths,
        ids,
        gates,
        gain,
        hidden,
        queries,
        new_keys,
        new_values,
        keys,
        values,
        o_weight,
        w_gate,
        w_up,
        w_down,
    )


def shuffle_matrix(back):
    one, other = (1, 0) if back else (0, 1)
    banded = iota((SHUFFLE, SHUFFLE), one)
    chunked = iota((SHUFFLE, SHUFFLE), other)
    same = (
        (banded // BAND == (chunked // SLOTS) % BLOCKS)
        & ((banded % BAND) // SLOTS == chunked // CHUNK_ROWS)
        & (banded % SLOTS == chunked % SLOTS)
    )
    return same.astype(F32).astype(BF16)


def expert_kernel(received_ref, gate_ref, up_ref, down_ref, out_ref, rows, inner):
    spread = shuffle_matrix(False)
    for b in range(SHUFFLES):
        part = dot(spread, received_ref[b * SHUFFLE : (b + 1) * SHUFFLE, :]).astype(BF16)
        for q in range(BLOCKS):
            rows[b * BAND : (b + 1) * BAND, q * CHUNK_COLS : (q + 1) * CHUNK_COLS] = part[
                q * BAND : (q + 1) * BAND, :
            ]
    for f in range(0, FF, FF_CHUNK):
        gate = dot(rows[...], gate_ref[:, f : f + FF_CHUNK])
        up = dot(rows[...], up_ref[:, f : f + FF_CHUNK])
        inner[:, f : f + FF_CHUNK] = (gate / (1.0 + jnp.exp(-gate)) * up).astype(BF16)
    for q in range(BLOCKS):
        cols = slice(q * CHUNK_COLS, (q + 1) * CHUNK_COLS)
        rows[:, cols] = dot(inner[...], down_ref[:, cols]).astype(BF16)
    gather = shuffle_matrix(True)
    for b in range(SHUFFLES):
        part = jnp.concatenate(
            [
                rows[b * BAND : (b + 1) * BAND, q * CHUNK_COLS : (q + 1) * CHUNK_COLS]
                for q in range(BLOCKS)
            ],
            axis=0,
        )
        out_ref[b * SHUFFLE : (b + 1) * SHUFFLE, :] = dot(gather, part).astype(BF16)


def expert_part(received, w_gate, w_up, w_down):
    count = EXPERTS * SLOTS
    return pl.pallas_call(
        expert_kernel,
        out_shape=pltpu.VMEM((LINES, CHUNK_COLS), BF16),
        in_specs=[VMEM] * 4,
        out_specs=VMEM,
        scratch_shapes=[pltpu.VMEM((count, D), BF16), pltpu.VMEM((count, FF), BF16)],
        compiler_params=pltpu.CompilerParams(vmem_limit_bytes=32 * MIB),
        cost_estimate=pl.CostEstimate(
            flops=6 * count * D * FF, bytes_accessed=12 * MIB, transcendentals=0
        ),
        name="experts",
    )(received, w_gate, w_up, w_down)


def combine_kernel(returned_ref, mixing_ref, after_ref, out_ref):
    mix = dot(mixing_ref[...], returned_ref[...])
    mix = mix[:TALL] + mix[TALL:]
    for q in range(BLOCKS):
        cols = slice(q * CHUNK_COLS, (q + 1) * CHUNK_COLS)
        out_ref[:, cols] = (
            after_ref[:, cols].astype(F32) + mix[q * ROWS_DEV : (q + 1) * ROWS_DEV, :]
        ).astype(BF16)


def combine(returned, mixing, after):
    return pl.pallas_call(
        combine_kernel,
        out_shape=jax.ShapeDtypeStruct((ROWS_DEV, D), BF16),
        in_specs=[VMEM] * 3,
        out_specs=VMEM,
        compiler_params=pltpu.CompilerParams(vmem_limit_bytes=24 * MIB),
        cost_estimate=pl.CostEstimate(
            flops=4 * TALL * LINES * CHUNK_COLS, bytes_accessed=4 * MIB, transcendentals=0
        ),
        name="combine",
    )(returned, mixing, after)


def exchange(array):
    return lax.all_to_all(
        array.reshape(EXPERTS, CHUNK_ROWS, CHUNK_COLS),
        ("sec", "dev"),
        split_axis=0,
        concat_axis=0,
        tiled=True,
    ).reshape(LINES, CHUNK_COLS)


def on_device(
    hidden_state,
    queries,
    new_keys,
    new_values,
    cache_keys,
    cache_values,
    lengths,
    o_weight,
    norm_gain,
    expert_ids,
    gate_values,
    w_gate,
    w_up,
    w_down,
):
    after, outgoing, mixing, *weights = attention_part(
        lengths,
        expert_ids.T,
        gate_values.T,
        norm_gain.reshape(1, D),
        hidden_state,
        queries,
        new_keys,
        new_values,
        cache_keys.reshape(-1, KV_HEADS * HEAD_DIM),
        cache_values.reshape(-1, KV_HEADS * HEAD_DIM),
        o_weight,
        w_gate.reshape(D, FF),
        w_up.reshape(D, FF),
        w_down.reshape(FF, D),
    )
    made = expert_part(exchange(outgoing), *weights)
    return combine(exchange(made), mixing, after)


def solution(mesh):
    split = ("sec", "dev")
    rows = P(split, None)
    stack = P(split, None, None)
    return jax.shard_map(
        on_device,
        mesh=mesh,
        in_specs=(
            rows,
            rows,
            rows,
            rows,
            stack,
            stack,
            P(split),
            P(),
            P(),
            rows,
            rows,
            stack,
            stack,
            stack,
        ),
        out_specs=rows,
        check_vma=False,
    )
```

```python
import math

import jax
import jax.numpy as jnp
from jax import lax
from jax.experimental import pallas as pl
from jax.experimental.pallas import tpu as pltpu
from jax.sharding import PartitionSpec as P

D = 2048
FF = 768
KV_HEADS = 2
HEAD_DIM = 128
GROUP = 8
TOP = 8
MICRO = 16
ROWS_DEV = 32
LMAX = 96
MOST = 2
EXPERTS = 128

SLOTS = MOST * ROWS_DEV // MICRO
CHUNK_ROWS = 16
CHUNK_COLS = SLOTS * D // CHUNK_ROWS
BLOCKS = CHUNK_ROWS // SLOTS
LINES = EXPERTS * CHUNK_ROWS
TALL = BLOCKS * ROWS_DEV

SUB = 8
GROUPS = ROWS_DEV // SUB
O_CHUNKS = 8
O_DEPTH = D // O_CHUNKS
WEIGHT_PARTS = 4
FF_CHUNK = 256

SHUFFLE = 256
SOURCES = SHUFFLE // CHUNK_ROWS
BAND = SOURCES * SLOTS
SHUFFLES = LINES // SHUFFLE

MIB = 2**20
F32 = jnp.float32
BF16 = jnp.bfloat16
NT = (((1,), (1,)), ((), ()))
VMEM = pl.BlockSpec(memory_space=pltpu.VMEM)
HBM = pl.BlockSpec(memory_space=pltpu.HBM)


def iota(shape, dim):
    return lax.broadcasted_iota(jnp.int32, shape, dim)


def dot(a, b):
    return jnp.dot(a, b, preferred_element_type=F32)


def tile_lanes(array):
    return jnp.concatenate([array] * BLOCKS, axis=1)


def slot_table(ids):
    ids = tile_lanes(ids)
    expert = iota((EXPERTS, TALL), 0)
    named = jnp.zeros((EXPERTS, TALL), F32)
    for k in range(TOP):
        named = jnp.where(ids[k : k + 1, :] == expert, 1.0, named)
    first, second = iota((TALL, TALL), 0), iota((TALL, TALL), 1)
    before = jnp.where((first // MICRO == second // MICRO) & (first < second), 1.0, 0.0)
    earlier = dot(named.astype(BF16), before.astype(BF16))
    micro = (iota((EXPERTS, TALL), 1) % ROWS_DEV) // MICRO
    return named * (earlier + (micro * MOST + 1).astype(F32))


def attend_group(group, lengths, queries, new_keys, new_values, keys, values, attended):
    scale = HEAD_DIM ** (-0.5) * math.log2(math.e)
    mine = pl.ds(group * SUB, SUB)
    query = queries[mine, :].astype(F32)
    own_key = new_keys[mine, :].astype(F32)
    own_value = new_values[mine, :].astype(F32)
    cache = pl.ds(group * SUB * LMAX, SUB * LMAX)
    row = iota((SUB, SUB * LMAX), 0)
    length = jnp.zeros((SUB, SUB * LMAX), jnp.int32)
    for r in range(SUB):
        length = jnp.where(row == r, lengths[group * SUB + r], length)
    place = iota((SUB, SUB * LMAX), 1) - row * LMAX
    bias = jnp.where((place >= 0) & (place < length), 0.0, -jnp.inf)
    bias = jnp.concatenate([bias] * GROUP, axis=0)
    for kv in range(KV_HEADS):
        cols = slice(kv * HEAD_DIM, (kv + 1) * HEAD_DIM)
        first = kv * GROUP * HEAD_DIM
        heads = jnp.concatenate(
            [query[:, first + g * HEAD_DIM : first + (g + 1) * HEAD_DIM] for g in range(GROUP)],
            axis=0,
        )
        key_tall = jnp.concatenate([own_key[:, cols]] * GROUP, axis=0)
        value_tall = jnp.concatenate([own_value[:, cols]] * GROUP, axis=0)
        scores = lax.dot_general(
            heads.astype(BF16), keys[cache, cols], NT, preferred_element_type=F32
        )
        scores = scores + bias
        own = jnp.sum(heads * key_tall, axis=1, keepdims=True)
        peak = jnp.maximum(jnp.max(scores, axis=1, keepdims=True), own)
        raw = jnp.exp2((scores - peak) * scale)
        raw_own = jnp.exp2((own - peak) * scale)
        share = 1.0 / (jnp.sum(raw, axis=1, keepdims=True) + raw_own)
        result = (dot(raw.astype(BF16), values[cache, cols]) + raw_own * value_tall) * share
        for g in range(GROUP):
            attended[mine, first + g * HEAD_DIM : first + (g + 1) * HEAD_DIM] = result[
                g * SUB : (g + 1) * SUB, :
            ]


def combine_weights(table, ids, gates):
    ids = tile_lanes(ids)
    gates = tile_lanes(gates)
    expert = iota((EXPERTS, TALL), 0)
    gate = jnp.zeros((EXPERTS, TALL), F32)
    for k in range(TOP):
        gate = jnp.where(ids[k : k + 1, :] == expert, gates[k : k + 1, :], gate)
    gate = jnp.transpose(gate)
    high = gate.astype(BF16)
    low = (gate - high.astype(F32)).astype(BF16)
    table = jnp.transpose(table).astype(BF16)
    lane = iota((EXPERTS, LINES), 1)
    spread = (lane // CHUNK_ROWS == iota((EXPERTS, LINES), 0)).astype(BF16)
    lane = iota((TALL, LINES), 1)
    wanted = jnp.where(
        (lane // SLOTS) % BLOCKS == iota((TALL, LINES), 0) // ROWS_DEV,
        (lane % SLOTS + 1).astype(F32),
        -1.0,
    )
    live = dot(table, spread) == wanted
    return [jnp.where(live, dot(part, spread), 0.0).astype(BF16) for part in (high, low)]


def dispatch_weights(table):
    line = iota((LINES, EXPERTS), 0)
    spread = (line // CHUNK_ROWS == iota((LINES, EXPERTS), 1)).astype(BF16)
    wanted = jnp.where(
        (line // SLOTS) % BLOCKS == iota((LINES, TALL), 1) // ROWS_DEV,
        (line % SLOTS + 1).astype(F32),
        -1.0,
    )
    return jnp.where(dot(spread, table.astype(BF16)) == wanted, 1.0, 0.0).astype(BF16)


def attention_kernel(
    lengths_hbm,
    ids_hbm,
    gates_hbm,
    gain_hbm,
    hidden_hbm,
    queries_hbm,
    new_keys_hbm,
    new_values_hbm,
    keys_hbm,
    values_hbm,
    o_hbm,
    gate_hbm,
    up_hbm,
    after_ref,
    outgoing_ref,
    mixing_ref,
    gate_ref,
    up_ref,
    lengths,
    ids,
    gates,
    gain,
    hidden,
    queries,
    new_keys,
    new_values,
    keys,
    values,
    o_weight,
    attended,
    dispatch,
    small_sem,
    key_sem,
    value_sem,
    o_sem,
    weight_sem,
):
    pairs = (
        (ids_hbm, ids),
        (gates_hbm, gates),
        (queries_hbm, queries),
        (new_keys_hbm, new_keys),
        (new_values_hbm, new_values),
        (lengths_hbm, lengths),
        (hidden_hbm, hidden),
        (gain_hbm, gain),
    )
    small = [
        pltpu.make_async_copy(source, target, small_sem.at[i])
        for i, (source, target) in enumerate(pairs)
    ]
    for copy in small:
        copy.start()
    key_copies, value_copies, o_copies = [], [], []
    for group in range(GROUPS):
        part = pl.ds(group * SUB * LMAX, SUB * LMAX)
        key_copies.append(
            pltpu.make_async_copy(keys_hbm.at[part], keys.at[part], key_sem.at[group])
        )
        value_copies.append(
            pltpu.make_async_copy(values_hbm.at[part], values.at[part], value_sem.at[group])
        )
        key_copies[group].start()
        value_copies[group].start()
    for c in range(O_CHUNKS):
        part = pl.ds(c * O_DEPTH, O_DEPTH)
        o_copies.append(pltpu.make_async_copy(o_hbm.at[part], o_weight.at[part], o_sem.at[c]))
    weight_copies = []
    for i, (source, target) in enumerate(
        ((gate_hbm, gate_ref), (up_hbm, up_ref))
    ):
        depth = source.shape[0] // WEIGHT_PARTS
        for c in range(WEIGHT_PARTS):
            part = pl.ds(c * depth, depth)
            weight_copies.append(
                pltpu.make_async_copy(source.at[part], target.at[part], weight_sem.at[i, c])
            )

    for copy in small[:2]:
        copy.wait()
    table = slot_table(ids[...])
    dispatch[...] = dispatch_weights(table)
    high, low = combine_weights(table, ids[...], gates[...])
    mixing_ref[:TALL, :] = high
    mixing_ref[TALL:, :] = low

    for copy in small[2:]:
        copy.wait()
    for group in range(GROUPS):
        if group % 2 == 0:
            for g in (group, group + 1):
                key_copies[g].wait()
                value_copies[g].wait()
            for copy in (o_copies, (), weight_copies, ())[group]:
                copy.start()
        attend_group(group, lengths, queries, new_keys, new_values, keys, values, attended)

    total = hidden[...].astype(F32)
    for c in range(O_CHUNKS):
        o_copies[c].wait()
        part = slice(c * O_DEPTH, (c + 1) * O_DEPTH)
        total = total + dot(attended[:, part].astype(BF16), o_weight[part, :])
    after = total.astype(BF16)
    after_ref[...] = after
    after = after.astype(F32)
    mean = jnp.mean(after * after, axis=1, keepdims=True)
    normed = (after * lax.rsqrt(mean + 1e-6) * gain[...]).astype(BF16)
    stacked = jnp.concatenate(
        [normed[:, q * CHUNK_COLS : (q + 1) * CHUNK_COLS] for q in range(BLOCKS)], axis=0
    )
    outgoing_ref[...] = dot(dispatch[...], stacked).astype(BF16)
    for copy in weight_copies:
        copy.wait()


def attention_part(
    lengths,
    ids,
    gates,
    gain,
    hidden,
    queries,
    new_keys,
    new_values,
    keys,
    values,
    o_weight,
    w_gate,
    w_up,
):
    cache = (ROWS_DEV * LMAX, KV_HEADS * HEAD_DIM)
    return pl.pallas_call(
        attention_kernel,
        out_shape=(
            pltpu.VMEM((ROWS_DEV, D), BF16),
            pltpu.VMEM((LINES, CHUNK_COLS), BF16),
            pltpu.VMEM((2 * TALL, LINES), BF16),
            pltpu.VMEM((D, FF), BF16),
            pltpu.VMEM((D, FF), BF16),
        ),
        in_specs=[HBM] * 13,
        out_specs=(VMEM,) * 5,
        scratch_shapes=[
            pltpu.SMEM((ROWS_DEV,), jnp.int32),
            pltpu.VMEM((TOP, ROWS_DEV), jnp.int32),
            pltpu.VMEM((TOP, ROWS_DEV), F32),
            pltpu.VMEM((1, D), F32),
            pltpu.VMEM((ROWS_DEV, D), BF16),
            pltpu.VMEM((ROWS_DEV, D), BF16),
            pltpu.VMEM((ROWS_DEV, KV_HEADS * HEAD_DIM), BF16),
            pltpu.VMEM((ROWS_DEV, KV_HEADS * HEAD_DIM), BF16),
            pltpu.VMEM(cache, BF16),
            pltpu.VMEM(cache, BF16),
            pltpu.VMEM((D, D), BF16),
            pltpu.VMEM((ROWS_DEV, D), F32),
            pltpu.VMEM((LINES, TALL), BF16),
            pltpu.SemaphoreType.DMA((8,)),
            pltpu.SemaphoreType.DMA((GROUPS,)),
            pltpu.SemaphoreType.DMA((GROUPS,)),
            pltpu.SemaphoreType.DMA((O_CHUNKS,)),
            pltpu.SemaphoreType.DMA((3, WEIGHT_PARTS)),
        ],
        compiler_params=pltpu.CompilerParams(vmem_limit_bytes=53 * MIB),
        cost_estimate=pl.CostEstimate(
            flops=2 * ROWS_DEV * D * D, bytes_accessed=16 * MIB, transcendentals=0
        ),
        name="attend",
    )(
        lengths,
        ids,
        gates,
        gain,
        hidden,
        queries,
        new_keys,
        new_values,
        keys,
        values,
        o_weight,
        w_gate,
        w_up,
    )


def shuffle_matrix(back):
    one, other = (1, 0) if back else (0, 1)
    banded = iota((SHUFFLE, SHUFFLE), one)
    chunked = iota((SHUFFLE, SHUFFLE), other)
    same = (
        (banded // BAND == (chunked // SLOTS) % BLOCKS)
        & ((banded % BAND) // SLOTS == chunked // CHUNK_ROWS)
        & (banded % SLOTS == chunked % SLOTS)
    )
    return same.astype(F32).astype(BF16)


def expert_kernel(received_ref, gate_ref, up_ref, down_ref, out_ref, rows, inner):
    spread = shuffle_matrix(False)
    for b in range(SHUFFLES):
        part = dot(spread, received_ref[b * SHUFFLE : (b + 1) * SHUFFLE, :]).astype(BF16)
        for q in range(BLOCKS):
            rows[b * BAND : (b + 1) * BAND, q * CHUNK_COLS : (q + 1) * CHUNK_COLS] = part[
                q * BAND : (q + 1) * BAND, :
            ]
    for f in range(0, FF, FF_CHUNK):
        gate = dot(rows[...], gate_ref[:, f : f + FF_CHUNK])
        up = dot(rows[...], up_ref[:, f : f + FF_CHUNK])
        inner[:, f : f + FF_CHUNK] = (gate / (1.0 + jnp.exp(-gate)) * up).astype(BF16)
    for q in range(BLOCKS):
        cols = slice(q * CHUNK_COLS, (q + 1) * CHUNK_COLS)
        rows[:, cols] = dot(inner[...], down_ref[:, cols]).astype(BF16)
    gather = shuffle_matrix(True)
    for b in range(SHUFFLES):
        part = jnp.concatenate(
            [
                rows[b * BAND : (b + 1) * BAND, q * CHUNK_COLS : (q + 1) * CHUNK_COLS]
                for q in range(BLOCKS)
            ],
            axis=0,
        )
        out_ref[b * SHUFFLE : (b + 1) * SHUFFLE, :] = dot(gather, part).astype(BF16)


def expert_part(received, w_gate, w_up, w_down):
    count = EXPERTS * SLOTS
    return pl.pallas_call(
        expert_kernel,
        out_shape=pltpu.VMEM((LINES, CHUNK_COLS), BF16),
        in_specs=[VMEM] * 4,
        out_specs=VMEM,
        scratch_shapes=[pltpu.VMEM((count, D), BF16), pltpu.VMEM((count, FF), BF16)],
        compiler_params=pltpu.CompilerParams(vmem_limit_bytes=32 * MIB),
        cost_estimate=pl.CostEstimate(
            flops=6 * count * D * FF, bytes_accessed=12 * MIB, transcendentals=0
        ),
        name="experts",
    )(received, w_gate, w_up, w_down)


def combine_kernel(returned_ref, mixing_ref, after_ref, out_ref):
    mix = dot(mixing_ref[...], returned_ref[...])
    mix = mix[:TALL] + mix[TALL:]
    for q in range(BLOCKS):
        cols = slice(q * CHUNK_COLS, (q + 1) * CHUNK_COLS)
        out_ref[:, cols] = (
            after_ref[:, cols].astype(F32) + mix[q * ROWS_DEV : (q + 1) * ROWS_DEV, :]
        ).astype(BF16)


def combine(returned, mixing, after):
    return pl.pallas_call(
        combine_kernel,
        out_shape=jax.ShapeDtypeStruct((ROWS_DEV, D), BF16),
        in_specs=[VMEM] * 3,
        out_specs=VMEM,
        compiler_params=pltpu.CompilerParams(vmem_limit_bytes=24 * MIB),
        cost_estimate=pl.CostEstimate(
            flops=4 * TALL * LINES * CHUNK_COLS, bytes_accessed=4 * MIB, transcendentals=0
        ),
        name="combine",
    )(returned, mixing, after)


def exchange(array):
    return lax.all_to_all(
        array.reshape(EXPERTS, CHUNK_ROWS, CHUNK_COLS),
        ("sec", "dev"),
        split_axis=0,
        concat_axis=0,
        tiled=True,
    ).reshape(LINES, CHUNK_COLS)


def on_device(
    hidden_state,
    queries,
    new_keys,
    new_values,
    cache_keys,
    cache_values,
    lengths,
    o_weight,
    norm_gain,
    expert_ids,
    gate_values,
    w_gate,
    w_up,
    w_down,
):
    after, outgoing, mixing, *weights = attention_part(
        lengths,
        expert_ids.T,
        gate_values.T,
        norm_gain.reshape(1, D),
        hidden_state,
        queries,
        new_keys,
        new_values,
        cache_keys.reshape(-1, KV_HEADS * HEAD_DIM),
        cache_values.reshape(-1, KV_HEADS * HEAD_DIM),
        o_weight,
        w_gate.reshape(D, FF),
        w_up.reshape(D, FF),
    )
    made = expert_part(exchange(outgoing), *weights, w_down.reshape(FF, D))
    return combine(exchange(made), mixing, after)


def solution(mesh):
    split = ("sec", "dev")
    rows = P(split, None)
    stack = P(split, None, None)
    return jax.shard_map(
        on_device,
        mesh=mesh,
        in_specs=(
            rows,
            rows,
            rows,
            rows,
            stack,
            stack,
            P(split),
            P(),
            P(),
            rows,
            rows,
            stack,
            stack,
            stack,
        ),
        out_specs=rows,
        check_vma=False,
    )
```

```python
import math

import jax
import jax.numpy as jnp
from jax import lax
from jax.experimental import pallas as pl
from jax.experimental.pallas import tpu as pltpu
from jax.sharding import PartitionSpec as P

D = 2048
FF = 768
KV_HEADS = 2
HEAD_DIM = 128
GROUP = 8
TOP = 8
MICRO = 16
ROWS_DEV = 32
LMAX = 96
MOST = 2
EXPERTS = 128

SLOTS = MOST * ROWS_DEV // MICRO
LINES = EXPERTS * SLOTS
COPIES = EXPERTS // ROWS_DEV

SUB = 8
GROUPS = ROWS_DEV // SUB
O_CHUNKS = 8
O_DEPTH = D // O_CHUNKS
WEIGHT_PARTS = 4
FF_CHUNK = 256

OUT_CHUNK = 512

MIB = 2**20
F32 = jnp.float32
BF16 = jnp.bfloat16
NT = (((1,), (1,)), ((), ()))
VMEM = pl.BlockSpec(memory_space=pltpu.VMEM)
HBM = pl.BlockSpec(memory_space=pltpu.HBM)


def iota(shape, dim):
    return lax.broadcasted_iota(jnp.int32, shape, dim)


def dot(a, b):
    return jnp.dot(a, b, preferred_element_type=F32)


def tile_lanes(array):
    return jnp.concatenate([array] * COPIES, axis=1)


def slot_table(ids):
    ids = tile_lanes(ids)
    square = (EXPERTS, EXPERTS)
    expert = iota(square, 0)
    named = jnp.zeros(square, F32)
    for k in range(TOP):
        named = jnp.where(ids[k : k + 1, :] == expert, 1.0, named)
    first, second = iota(square, 0), iota(square, 1)
    before = jnp.where((first // MICRO == second // MICRO) & (first < second), 1.0, 0.0)
    earlier = dot(named.astype(BF16), before.astype(BF16))
    micro = (iota(square, 1) % ROWS_DEV) // MICRO
    return named * (earlier + (micro * MOST + 1).astype(F32))


def attend_group(group, lengths, queries, new_keys, new_values, keys, values, attended):
    scale = HEAD_DIM ** (-0.5) * math.log2(math.e)
    mine = pl.ds(group * SUB, SUB)
    query = queries[mine, :].astype(F32)
    own_key = new_keys[mine, :].astype(F32)
    own_value = new_values[mine, :].astype(F32)
    cache = pl.ds(group * SUB * LMAX, SUB * LMAX)
    row = iota((SUB, SUB * LMAX), 0)
    length = jnp.zeros((SUB, SUB * LMAX), jnp.int32)
    for r in range(SUB):
        length = jnp.where(row == r, lengths[group * SUB + r], length)
    place = iota((SUB, SUB * LMAX), 1) - row * LMAX
    bias = jnp.where((place >= 0) & (place < length), 0.0, -jnp.inf)
    bias = jnp.concatenate([bias] * GROUP, axis=0)
    for kv in range(KV_HEADS):
        cols = slice(kv * HEAD_DIM, (kv + 1) * HEAD_DIM)
        first = kv * GROUP * HEAD_DIM
        heads = jnp.concatenate(
            [query[:, first + g * HEAD_DIM : first + (g + 1) * HEAD_DIM] for g in range(GROUP)],
            axis=0,
        )
        key_tall = jnp.concatenate([own_key[:, cols]] * GROUP, axis=0)
        value_tall = jnp.concatenate([own_value[:, cols]] * GROUP, axis=0)
        scores = lax.dot_general(
            heads.astype(BF16), keys[cache, cols], NT, preferred_element_type=F32
        )
        scores = scores + bias
        own = jnp.sum(heads * key_tall, axis=1, keepdims=True)
        peak = jnp.maximum(jnp.max(scores, axis=1, keepdims=True), own)
        raw = jnp.exp2((scores - peak) * scale)
        raw_own = jnp.exp2((own - peak) * scale)
        share = 1.0 / (jnp.sum(raw, axis=1, keepdims=True) + raw_own)
        result = (dot(raw.astype(BF16), values[cache, cols]) + raw_own * value_tall) * share
        for g in range(GROUP):
            attended[mine, first + g * HEAD_DIM : first + (g + 1) * HEAD_DIM] = result[
                g * SUB : (g + 1) * SUB, :
            ]


def combine_weights(table, ids, gates):
    ids = tile_lanes(ids)
    gates = tile_lanes(gates)
    expert = iota((EXPERTS, EXPERTS), 0)
    gate = jnp.zeros((EXPERTS, EXPERTS), F32)
    for k in range(TOP):
        gate = jnp.where(ids[k : k + 1, :] == expert, gates[k : k + 1, :], gate)
    gate = jnp.transpose(gate)[:ROWS_DEV]
    high = gate.astype(BF16)
    low = (gate - high.astype(F32)).astype(BF16)
    table = jnp.transpose(table)[:ROWS_DEV].astype(BF16)
    spread = (iota((EXPERTS, LINES), 1) // SLOTS == iota((EXPERTS, LINES), 0)).astype(BF16)
    wanted = (iota((ROWS_DEV, LINES), 1) % SLOTS + 1).astype(F32)
    live = dot(table, spread) == wanted
    return [jnp.where(live, dot(part, spread), 0.0).astype(BF16) for part in (high, low)]


def dispatch_weights(table):
    spread = (iota((LINES, EXPERTS), 0) // SLOTS == iota((LINES, EXPERTS), 1)).astype(BF16)
    wanted = (iota((LINES, EXPERTS), 0) % SLOTS + 1).astype(F32)
    full = jnp.where(dot(spread, table.astype(BF16)) == wanted, 1.0, 0.0)
    return full[:, :ROWS_DEV].astype(BF16)


def attention_kernel(
    lengths_hbm,
    ids_hbm,
    gates_hbm,
    gain_hbm,
    hidden_hbm,
    queries_hbm,
    new_keys_hbm,
    new_values_hbm,
    keys_hbm,
    values_hbm,
    o_hbm,
    gate_hbm,
    up_hbm,
    after_ref,
    outgoing_ref,
    mixing_ref,
    gate_ref,
    up_ref,
    lengths,
    ids,
    gates,
    gain,
    hidden,
    queries,
    new_keys,
    new_values,
    keys,
    values,
    o_weight,
    attended,
    dispatch,
    small_sem,
    key_sem,
    value_sem,
    o_sem,
    weight_sem,
):
    pairs = (
        (ids_hbm, ids),
        (gates_hbm, gates),
        (queries_hbm, queries),
        (new_keys_hbm, new_keys),
        (new_values_hbm, new_values),
        (lengths_hbm, lengths),
        (hidden_hbm, hidden),
        (gain_hbm, gain),
    )
    small = [
        pltpu.make_async_copy(source, target, small_sem.at[i])
        for i, (source, target) in enumerate(pairs)
    ]
    for copy in small:
        copy.start()
    key_copies, value_copies, o_copies = [], [], []
    for group in range(GROUPS):
        part = pl.ds(group * SUB * LMAX, SUB * LMAX)
        key_copies.append(
            pltpu.make_async_copy(keys_hbm.at[part], keys.at[part], key_sem.at[group])
        )
        value_copies.append(
            pltpu.make_async_copy(values_hbm.at[part], values.at[part], value_sem.at[group])
        )
        key_copies[group].start()
        value_copies[group].start()
    for c in range(O_CHUNKS):
        part = pl.ds(c * O_DEPTH, O_DEPTH)
        o_copies.append(pltpu.make_async_copy(o_hbm.at[part], o_weight.at[part], o_sem.at[c]))
    weight_copies = []
    for i, (source, target) in enumerate(
        ((gate_hbm, gate_ref), (up_hbm, up_ref))
    ):
        depth = source.shape[0] // WEIGHT_PARTS
        for c in range(WEIGHT_PARTS):
            part = pl.ds(c * depth, depth)
            weight_copies.append(
                pltpu.make_async_copy(source.at[part], target.at[part], weight_sem.at[i, c])
            )

    for copy in small[:2]:
        copy.wait()
    table = slot_table(ids[...])
    dispatch[...] = dispatch_weights(table)
    high, low = combine_weights(table, ids[...], gates[...])
    mixing_ref[:ROWS_DEV, :] = high
    mixing_ref[ROWS_DEV:, :] = low

    for copy in o_copies:
        copy.start()
    for copy in small[2:]:
        copy.wait()
    for group in range(GROUPS):
        if group % 2 == 0:
            for g in (group, group + 1):
                key_copies[g].wait()
                value_copies[g].wait()
            for copy in ((), (), weight_copies, ())[group]:
                copy.start()
        attend_group(group, lengths, queries, new_keys, new_values, keys, values, attended)

    total = hidden[...].astype(F32)
    for c in range(O_CHUNKS):
        o_copies[c].wait()
        part = slice(c * O_DEPTH, (c + 1) * O_DEPTH)
        total = total + dot(attended[:, part].astype(BF16), o_weight[part, :])
    after = total.astype(BF16)
    after_ref[...] = after
    after = after.astype(F32)
    mean = jnp.mean(after * after, axis=1, keepdims=True)
    normed = (after * lax.rsqrt(mean + 1e-6) * gain[...]).astype(BF16)
    for c in range(0, D, OUT_CHUNK):
        part = dot(dispatch[...], normed[:, c : c + OUT_CHUNK]).astype(BF16)
        outgoing_ref[:, :, c : c + OUT_CHUNK] = part.reshape(EXPERTS, SLOTS, OUT_CHUNK)
    for copy in weight_copies:
        copy.wait()


def attention_part(
    lengths,
    ids,
    gates,
    gain,
    hidden,
    queries,
    new_keys,
    new_values,
    keys,
    values,
    o_weight,
    w_gate,
    w_up,
):
    cache = (ROWS_DEV * LMAX, KV_HEADS * HEAD_DIM)
    return pl.pallas_call(
        attention_kernel,
        out_shape=(
            pltpu.VMEM((ROWS_DEV, D), BF16),
            pltpu.VMEM((EXPERTS, SLOTS, D), BF16),
            pltpu.VMEM((2 * ROWS_DEV, LINES), BF16),
            pltpu.VMEM((D, FF), BF16),
            pltpu.VMEM((D, FF), BF16),
        ),
        in_specs=[HBM] * 13,
        out_specs=(VMEM,) * 5,
        scratch_shapes=[
            pltpu.SMEM((ROWS_DEV,), jnp.int32),
            pltpu.VMEM((TOP, ROWS_DEV), jnp.int32),
            pltpu.VMEM((TOP, ROWS_DEV), F32),
            pltpu.VMEM((1, D), F32),
            pltpu.VMEM((ROWS_DEV, D), BF16),
            pltpu.VMEM((ROWS_DEV, D), BF16),
            pltpu.VMEM((ROWS_DEV, KV_HEADS * HEAD_DIM), BF16),
            pltpu.VMEM((ROWS_DEV, KV_HEADS * HEAD_DIM), BF16),
            pltpu.VMEM(cache, BF16),
            pltpu.VMEM(cache, BF16),
            pltpu.VMEM((D, D), BF16),
            pltpu.VMEM((ROWS_DEV, D), F32),
            pltpu.VMEM((LINES, ROWS_DEV), BF16),
            pltpu.SemaphoreType.DMA((8,)),
            pltpu.SemaphoreType.DMA((GROUPS,)),
            pltpu.SemaphoreType.DMA((GROUPS,)),
            pltpu.SemaphoreType.DMA((O_CHUNKS,)),
            pltpu.SemaphoreType.DMA((3, WEIGHT_PARTS)),
        ],
        compiler_params=pltpu.CompilerParams(vmem_limit_bytes=53 * MIB),
        cost_estimate=pl.CostEstimate(
            flops=2 * ROWS_DEV * D * D, bytes_accessed=16 * MIB, transcendentals=0
        ),
        name="attend",
    )(
        lengths,
        ids,
        gates,
        gain,
        hidden,
        queries,
        new_keys,
        new_values,
        keys,
        values,
        o_weight,
        w_gate,
        w_up,
    )


def expert_kernel(received_ref, gate_ref, up_ref, down_ref, out_ref, rows, inner):
    rows[...] = received_ref[...].reshape(LINES, D)
    for f in range(0, FF, FF_CHUNK):
        gate = dot(rows[...], gate_ref[:, f : f + FF_CHUNK])
        up = dot(rows[...], up_ref[:, f : f + FF_CHUNK])
        inner[:, f : f + FF_CHUNK] = (gate / (1.0 + jnp.exp(-gate)) * up).astype(BF16)
    for c in range(0, D, OUT_CHUNK):
        part = dot(inner[...], down_ref[:, c : c + OUT_CHUNK]).astype(BF16)
        out_ref[:, :, c : c + OUT_CHUNK] = part.reshape(EXPERTS, SLOTS, OUT_CHUNK)


def expert_part(received, w_gate, w_up, w_down):
    return pl.pallas_call(
        expert_kernel,
        out_shape=pltpu.VMEM((EXPERTS, SLOTS, D), BF16),
        in_specs=[VMEM] * 4,
        out_specs=VMEM,
        scratch_shapes=[pltpu.VMEM((LINES, D), BF16), pltpu.VMEM((LINES, FF), BF16)],
        compiler_params=pltpu.CompilerParams(vmem_limit_bytes=32 * MIB),
        cost_estimate=pl.CostEstimate(
            flops=6 * LINES * D * FF, bytes_accessed=12 * MIB, transcendentals=0
        ),
        name="experts",
    )(received, w_gate, w_up, w_down)


def combine_kernel(returned_ref, mixing_ref, after_ref, out_ref):
    for c in range(0, D, OUT_CHUNK):
        cols = slice(c, c + OUT_CHUNK)
        mix = dot(mixing_ref[...], returned_ref[:, :, cols].reshape(LINES, OUT_CHUNK))
        mix = mix[:ROWS_DEV] + mix[ROWS_DEV:]
        out_ref[:, cols] = (after_ref[:, cols].astype(F32) + mix).astype(BF16)


def combine(returned, mixing, after):
    return pl.pallas_call(
        combine_kernel,
        out_shape=jax.ShapeDtypeStruct((ROWS_DEV, D), BF16),
        in_specs=[VMEM] * 3,
        out_specs=VMEM,
        compiler_params=pltpu.CompilerParams(vmem_limit_bytes=24 * MIB),
        cost_estimate=pl.CostEstimate(
            flops=4 * ROWS_DEV * LINES * D, bytes_accessed=4 * MIB, transcendentals=0
        ),
        name="combine",
    )(returned, mixing, after)


def exchange(array):
    return lax.all_to_all(array, ("sec", "dev"), split_axis=0, concat_axis=0, tiled=True)


def on_device(
    hidden_state,
    queries,
    new_keys,
    new_values,
    cache_keys,
    cache_values,
    lengths,
    o_weight,
    norm_gain,
    expert_ids,
    gate_values,
    w_gate,
    w_up,
    w_down,
):
    after, outgoing, mixing, *weights = attention_part(
        lengths,
        expert_ids.T,
        gate_values.T,
        norm_gain.reshape(1, D),
        hidden_state,
        queries,
        new_keys,
        new_values,
        cache_keys.reshape(-1, KV_HEADS * HEAD_DIM),
        cache_values.reshape(-1, KV_HEADS * HEAD_DIM),
        o_weight,
        w_gate.reshape(D, FF),
        w_up.reshape(D, FF),
    )
    made = expert_part(exchange(outgoing), *weights, w_down.reshape(FF, D))
    return combine(exchange(made), mixing, after)


def solution(mesh):
    split = ("sec", "dev")
    rows = P(split, None)
    stack = P(split, None, None)
    return jax.shard_map(
        on_device,
        mesh=mesh,
        in_specs=(
            rows,
            rows,
            rows,
            rows,
            stack,
            stack,
            P(split),
            P(),
            P(),
            rows,
            rows,
            stack,
            stack,
            stack,
        ),
        out_specs=rows,
        check_vma=False,
    )
```

```python
import math

import jax
import jax.numpy as jnp
from jax import lax
from jax.experimental import pallas as pl
from jax.experimental.pallas import tpu as pltpu
from jax.sharding import PartitionSpec as P

D = 2048
FF = 768
KV_HEADS = 2
HEAD_DIM = 128
GROUP = 8
TOP = 8
MICRO = 16
ROWS_DEV = 32
LMAX = 96
MOST = 2
EXPERTS = 128

SLOTS = MOST * ROWS_DEV // MICRO
LINES = EXPERTS * SLOTS
COPIES = EXPERTS // ROWS_DEV

SUB = 8
GROUPS = ROWS_DEV // SUB
HALVES = 2
O_CHUNKS = 4
O_DEPTH = D // O_CHUNKS
WEIGHT_PARTS = 1
FF_CHUNK = 256

OUT_CHUNK = 512

MIB = 2**20
F32 = jnp.float32
BF16 = jnp.bfloat16
NT = (((1,), (1,)), ((), ()))
VMEM = pl.BlockSpec(memory_space=pltpu.VMEM)
HBM = pl.BlockSpec(memory_space=pltpu.HBM)


def iota(shape, dim):
    return lax.broadcasted_iota(jnp.int32, shape, dim)


def dot(a, b):
    return jnp.dot(a, b, preferred_element_type=F32)


def tile_lanes(array):
    return jnp.concatenate([array] * COPIES, axis=1)


def slot_table(ids):
    ids = tile_lanes(ids)
    square = (EXPERTS, EXPERTS)
    expert = iota(square, 0)
    named = jnp.zeros(square, F32)
    for k in range(TOP):
        named = jnp.where(ids[k : k + 1, :] == expert, 1.0, named)
    first, second = iota(square, 0), iota(square, 1)
    before = jnp.where((first // MICRO == second // MICRO) & (first < second), 1.0, 0.0)
    earlier = dot(named.astype(BF16), before.astype(BF16))
    micro = (iota(square, 1) % ROWS_DEV) // MICRO
    return named * (earlier + (micro * MOST + 1).astype(F32))


def attend_group(group, lengths, queries, new_keys, new_values, keys, values, attended):
    scale = HEAD_DIM ** (-0.5) * math.log2(math.e)
    mine = pl.ds(group * SUB, SUB)
    query = queries[mine, :].astype(F32)
    own_key = new_keys[mine, :].astype(F32)
    own_value = new_values[mine, :].astype(F32)
    cache = pl.ds(group * SUB * LMAX, SUB * LMAX)
    row = iota((SUB, SUB * LMAX), 0)
    length = jnp.zeros((SUB, SUB * LMAX), jnp.int32)
    for r in range(SUB):
        length = jnp.where(row == r, lengths[group * SUB + r], length)
    place = iota((SUB, SUB * LMAX), 1) - row * LMAX
    bias = jnp.where((place >= 0) & (place < length), 0.0, -jnp.inf)
    bias = jnp.concatenate([bias] * GROUP, axis=0)
    for kv in range(KV_HEADS):
        cols = slice(kv * HEAD_DIM, (kv + 1) * HEAD_DIM)
        first = kv * GROUP * HEAD_DIM
        heads = jnp.concatenate(
            [query[:, first + g * HEAD_DIM : first + (g + 1) * HEAD_DIM] for g in range(GROUP)],
            axis=0,
        )
        key_tall = jnp.concatenate([own_key[:, cols]] * GROUP, axis=0)
        value_tall = jnp.concatenate([own_value[:, cols]] * GROUP, axis=0)
        scores = lax.dot_general(
            heads.astype(BF16), keys[cache, cols], NT, preferred_element_type=F32
        )
        scores = scores + bias
        own = jnp.sum(heads * key_tall, axis=1, keepdims=True)
        peak = jnp.maximum(jnp.max(scores, axis=1, keepdims=True), own)
        raw = jnp.exp2((scores - peak) * scale)
        raw_own = jnp.exp2((own - peak) * scale)
        share = 1.0 / (jnp.sum(raw, axis=1, keepdims=True) + raw_own)
        result = (dot(raw.astype(BF16), values[cache, cols]) + raw_own * value_tall) * share
        for g in range(GROUP):
            attended[mine, first + g * HEAD_DIM : first + (g + 1) * HEAD_DIM] = result[
                g * SUB : (g + 1) * SUB, :
            ]


def combine_weights(table, ids, gates):
    ids = tile_lanes(ids)
    gates = tile_lanes(gates)
    expert = iota((EXPERTS, EXPERTS), 0)
    gate = jnp.zeros((EXPERTS, EXPERTS), F32)
    for k in range(TOP):
        gate = jnp.where(ids[k : k + 1, :] == expert, gates[k : k + 1, :], gate)
    gate = jnp.transpose(gate)[:ROWS_DEV]
    high = gate.astype(BF16)
    low = (gate - high.astype(F32)).astype(BF16)
    table = jnp.transpose(table)[:ROWS_DEV].astype(BF16)
    spread = (iota((EXPERTS, LINES), 1) // SLOTS == iota((EXPERTS, LINES), 0)).astype(BF16)
    wanted = (iota((ROWS_DEV, LINES), 1) % SLOTS + 1).astype(F32)
    live = dot(table, spread) == wanted
    return [jnp.where(live, dot(part, spread), 0.0).astype(BF16) for part in (high, low)]


def dispatch_weights(table):
    spread = (iota((LINES, EXPERTS), 0) // SLOTS == iota((LINES, EXPERTS), 1)).astype(BF16)
    wanted = (iota((LINES, EXPERTS), 0) % SLOTS + 1).astype(F32)
    full = jnp.where(dot(spread, table.astype(BF16)) == wanted, 1.0, 0.0)
    return full[:, :ROWS_DEV].astype(BF16)


def attention_kernel(
    lengths_hbm,
    ids_hbm,
    gates_hbm,
    gain_hbm,
    hidden_hbm,
    queries_hbm,
    new_keys_hbm,
    new_values_hbm,
    keys_hbm,
    values_hbm,
    o_hbm,
    gate_hbm,
    up_hbm,
    after_ref,
    outgoing_ref,
    mixing_ref,
    gate_ref,
    up_ref,
    lengths,
    ids,
    gates,
    gain,
    hidden,
    queries,
    new_keys,
    new_values,
    keys,
    values,
    o_weight,
    attended,
    dispatch,
    small_sem,
    key_sem,
    value_sem,
    o_sem,
    weight_sem,
):
    pairs = (
        (ids_hbm, ids),
        (gates_hbm, gates),
        (queries_hbm, queries),
        (new_keys_hbm, new_keys),
        (new_values_hbm, new_values),
        (lengths_hbm, lengths),
        (hidden_hbm, hidden),
        (gain_hbm, gain),
    )
    small = [
        pltpu.make_async_copy(source, target, small_sem.at[i])
        for i, (source, target) in enumerate(pairs)
    ]
    for copy in small:
        copy.start()
    key_copies, value_copies, o_copies = [], [], []
    depth = ROWS_DEV * LMAX // HALVES
    for half in range(HALVES):
        part = pl.ds(half * depth, depth)
        key_copies.append(
            pltpu.make_async_copy(keys_hbm.at[part], keys.at[part], key_sem.at[half])
        )
        value_copies.append(
            pltpu.make_async_copy(values_hbm.at[part], values.at[part], value_sem.at[half])
        )
        key_copies[half].start()
        value_copies[half].start()
    for c in range(O_CHUNKS):
        part = pl.ds(c * O_DEPTH, O_DEPTH)
        o_copies.append(pltpu.make_async_copy(o_hbm.at[part], o_weight.at[part], o_sem.at[c]))
    weight_copies = []
    for i, (source, target) in enumerate(
        ((gate_hbm, gate_ref), (up_hbm, up_ref))
    ):
        depth = source.shape[0] // WEIGHT_PARTS
        for c in range(WEIGHT_PARTS):
            part = pl.ds(c * depth, depth)
            weight_copies.append(
                pltpu.make_async_copy(source.at[part], target.at[part], weight_sem.at[i, c])
            )

    for copy in small[:2]:
        copy.wait()
    table = slot_table(ids[...])
    dispatch[...] = dispatch_weights(table)
    high, low = combine_weights(table, ids[...], gates[...])
    mixing_ref[:ROWS_DEV, :] = high
    mixing_ref[ROWS_DEV:, :] = low

    for copy in o_copies:
        copy.start()
    for copy in small[2:]:
        copy.wait()
    for group in range(GROUPS):
        half, later = divmod(group, GROUPS // HALVES)
        if later == 0:
            key_copies[half].wait()
            value_copies[half].wait()
            for copy in ((), weight_copies)[half]:
                copy.start()
        attend_group(group, lengths, queries, new_keys, new_values, keys, values, attended)

    total = hidden[...].astype(F32)
    for c in range(O_CHUNKS):
        o_copies[c].wait()
        part = slice(c * O_DEPTH, (c + 1) * O_DEPTH)
        total = total + dot(attended[:, part].astype(BF16), o_weight[part, :])
    after = total.astype(BF16)
    after_ref[...] = after
    after = after.astype(F32)
    mean = jnp.mean(after * after, axis=1, keepdims=True)
    normed = (after * lax.rsqrt(mean + 1e-6) * gain[...]).astype(BF16)
    for c in range(0, D, OUT_CHUNK):
        part = dot(dispatch[...], normed[:, c : c + OUT_CHUNK]).astype(BF16)
        outgoing_ref[:, :, c : c + OUT_CHUNK] = part.reshape(EXPERTS, SLOTS, OUT_CHUNK)
    for copy in weight_copies:
        copy.wait()


def attention_part(
    lengths,
    ids,
    gates,
    gain,
    hidden,
    queries,
    new_keys,
    new_values,
    keys,
    values,
    o_weight,
    w_gate,
    w_up,
):
    cache = (ROWS_DEV * LMAX, KV_HEADS * HEAD_DIM)
    return pl.pallas_call(
        attention_kernel,
        out_shape=(
            pltpu.VMEM((ROWS_DEV, D), BF16),
            pltpu.VMEM((EXPERTS, SLOTS, D), BF16),
            pltpu.VMEM((2 * ROWS_DEV, LINES), BF16),
            pltpu.VMEM((D, FF), BF16),
            pltpu.VMEM((D, FF), BF16),
        ),
        in_specs=[HBM] * 13,
        out_specs=(VMEM,) * 5,
        scratch_shapes=[
            pltpu.SMEM((ROWS_DEV,), jnp.int32),
            pltpu.VMEM((TOP, ROWS_DEV), jnp.int32),
            pltpu.VMEM((TOP, ROWS_DEV), F32),
            pltpu.VMEM((1, D), F32),
            pltpu.VMEM((ROWS_DEV, D), BF16),
            pltpu.VMEM((ROWS_DEV, D), BF16),
            pltpu.VMEM((ROWS_DEV, KV_HEADS * HEAD_DIM), BF16),
            pltpu.VMEM((ROWS_DEV, KV_HEADS * HEAD_DIM), BF16),
            pltpu.VMEM(cache, BF16),
            pltpu.VMEM(cache, BF16),
            pltpu.VMEM((D, D), BF16),
            pltpu.VMEM((ROWS_DEV, D), F32),
            pltpu.VMEM((LINES, ROWS_DEV), BF16),
            pltpu.SemaphoreType.DMA((8,)),
            pltpu.SemaphoreType.DMA((HALVES,)),
            pltpu.SemaphoreType.DMA((HALVES,)),
            pltpu.SemaphoreType.DMA((O_CHUNKS,)),
            pltpu.SemaphoreType.DMA((3, WEIGHT_PARTS)),
        ],
        compiler_params=pltpu.CompilerParams(vmem_limit_bytes=53 * MIB),
        cost_estimate=pl.CostEstimate(
            flops=2 * ROWS_DEV * D * D, bytes_accessed=16 * MIB, transcendentals=0
        ),
        name="attend",
    )(
        lengths,
        ids,
        gates,
        gain,
        hidden,
        queries,
        new_keys,
        new_values,
        keys,
        values,
        o_weight,
        w_gate,
        w_up,
    )


def expert_kernel(received_ref, gate_ref, up_ref, down_ref, out_ref, rows, inner):
    rows[...] = received_ref[...].reshape(LINES, D)
    for f in range(0, FF, FF_CHUNK):
        gate = dot(rows[...], gate_ref[:, f : f + FF_CHUNK])
        up = dot(rows[...], up_ref[:, f : f + FF_CHUNK])
        inner[:, f : f + FF_CHUNK] = (gate / (1.0 + jnp.exp(-gate)) * up).astype(BF16)
    for c in range(0, D, OUT_CHUNK):
        part = dot(inner[...], down_ref[:, c : c + OUT_CHUNK]).astype(BF16)
        out_ref[:, :, c : c + OUT_CHUNK] = part.reshape(EXPERTS, SLOTS, OUT_CHUNK)


def expert_part(received, w_gate, w_up, w_down):
    return pl.pallas_call(
        expert_kernel,
        out_shape=pltpu.VMEM((EXPERTS, SLOTS, D), BF16),
        in_specs=[VMEM] * 4,
        out_specs=VMEM,
        scratch_shapes=[pltpu.VMEM((LINES, D), BF16), pltpu.VMEM((LINES, FF), BF16)],
        compiler_params=pltpu.CompilerParams(vmem_limit_bytes=32 * MIB),
        cost_estimate=pl.CostEstimate(
            flops=6 * LINES * D * FF, bytes_accessed=12 * MIB, transcendentals=0
        ),
        name="experts",
    )(received, w_gate, w_up, w_down)


def combine_kernel(returned_ref, mixing_ref, after_ref, out_ref):
    for c in range(0, D, OUT_CHUNK):
        cols = slice(c, c + OUT_CHUNK)
        mix = dot(mixing_ref[...], returned_ref[:, :, cols].reshape(LINES, OUT_CHUNK))
        mix = mix[:ROWS_DEV] + mix[ROWS_DEV:]
        out_ref[:, cols] = (after_ref[:, cols].astype(F32) + mix).astype(BF16)


def combine(returned, mixing, after):
    return pl.pallas_call(
        combine_kernel,
        out_shape=jax.ShapeDtypeStruct((ROWS_DEV, D), BF16),
        in_specs=[VMEM] * 3,
        out_specs=VMEM,
        compiler_params=pltpu.CompilerParams(vmem_limit_bytes=24 * MIB),
        cost_estimate=pl.CostEstimate(
            flops=4 * ROWS_DEV * LINES * D, bytes_accessed=4 * MIB, transcendentals=0
        ),
        name="combine",
    )(returned, mixing, after)


def exchange(array):
    return lax.all_to_all(array, ("sec", "dev"), split_axis=0, concat_axis=0, tiled=True)


def on_device(
    hidden_state,
    queries,
    new_keys,
    new_values,
    cache_keys,
    cache_values,
    lengths,
    o_weight,
    norm_gain,
    expert_ids,
    gate_values,
    w_gate,
    w_up,
    w_down,
):
    after, outgoing, mixing, *weights = attention_part(
        lengths,
        expert_ids.T,
        gate_values.T,
        norm_gain.reshape(1, D),
        hidden_state,
        queries,
        new_keys,
        new_values,
        cache_keys.reshape(-1, KV_HEADS * HEAD_DIM),
        cache_values.reshape(-1, KV_HEADS * HEAD_DIM),
        o_weight,
        w_gate.reshape(D, FF),
        w_up.reshape(D, FF),
    )
    made = expert_part(exchange(outgoing), *weights, w_down.reshape(FF, D))
    return combine(exchange(made), mixing, after)


def solution(mesh):
    split = ("sec", "dev")
    rows = P(split, None)
    stack = P(split, None, None)
    return jax.shard_map(
        on_device,
        mesh=mesh,
        in_specs=(
            rows,
            rows,
            rows,
            rows,
            stack,
            stack,
            P(split),
            P(),
            P(),
            rows,
            rows,
            stack,
            stack,
            stack,
        ),
        out_specs=rows,
        check_vma=False,
    )
```

```python
import math

import jax
import jax.numpy as jnp
from jax import lax
from jax.experimental import pallas as pl
from jax.experimental.pallas import tpu as pltpu
from jax.sharding import PartitionSpec as P

D = 2048
FF = 768
KV_HEADS = 2
HEAD_DIM = 128
GROUP = 8
TOP = 8
MICRO = 16
ROWS_DEV = 32
LMAX = 96
MOST = 2
EXPERTS = 128

SLOTS = MOST * ROWS_DEV // MICRO
LINES = EXPERTS * SLOTS
COPIES = EXPERTS // ROWS_DEV

SUB = 8
GROUPS = ROWS_DEV // SUB
HALVES = 2
O_CHUNKS = 4
O_DEPTH = D // O_CHUNKS
WEIGHT_PARTS = 1
FF_CHUNK = 256
EXPERT_PARTS = 2

OUT_CHUNK = 512

MIB = 2**20
F32 = jnp.float32
BF16 = jnp.bfloat16
NT = (((1,), (1,)), ((), ()))
VMEM = pl.BlockSpec(memory_space=pltpu.VMEM)
HBM = pl.BlockSpec(memory_space=pltpu.HBM)


def iota(shape, dim):
    return lax.broadcasted_iota(jnp.int32, shape, dim)


def dot(a, b):
    return jnp.dot(a, b, preferred_element_type=F32)


def tile_lanes(array):
    return jnp.concatenate([array] * COPIES, axis=1)


def slot_table(ids):
    ids = tile_lanes(ids)
    square = (EXPERTS, EXPERTS)
    expert = iota(square, 0)
    named = jnp.zeros(square, F32)
    for k in range(TOP):
        named = jnp.where(ids[k : k + 1, :] == expert, 1.0, named)
    first, second = iota(square, 0), iota(square, 1)
    before = jnp.where((first // MICRO == second // MICRO) & (first < second), 1.0, 0.0)
    earlier = dot(named.astype(BF16), before.astype(BF16))
    micro = (iota(square, 1) % ROWS_DEV) // MICRO
    return named * (earlier + (micro * MOST + 1).astype(F32))


def attend_group(group, lengths, queries, new_keys, new_values, keys, values, attended):
    scale = HEAD_DIM ** (-0.5) * math.log2(math.e)
    mine = pl.ds(group * SUB, SUB)
    query = queries[mine, :].astype(F32)
    own_key = new_keys[mine, :].astype(F32)
    own_value = new_values[mine, :].astype(F32)
    cache = pl.ds(group * SUB * LMAX, SUB * LMAX)
    row = iota((SUB, SUB * LMAX), 0)
    length = jnp.zeros((SUB, SUB * LMAX), jnp.int32)
    for r in range(SUB):
        length = jnp.where(row == r, lengths[group * SUB + r], length)
    place = iota((SUB, SUB * LMAX), 1) - row * LMAX
    bias = jnp.where((place >= 0) & (place < length), 0.0, -jnp.inf)
    bias = jnp.concatenate([bias] * GROUP, axis=0)
    for kv in range(KV_HEADS):
        cols = slice(kv * HEAD_DIM, (kv + 1) * HEAD_DIM)
        first = kv * GROUP * HEAD_DIM
        heads = jnp.concatenate(
            [query[:, first + g * HEAD_DIM : first + (g + 1) * HEAD_DIM] for g in range(GROUP)],
            axis=0,
        )
        key_tall = jnp.concatenate([own_key[:, cols]] * GROUP, axis=0)
        value_tall = jnp.concatenate([own_value[:, cols]] * GROUP, axis=0)
        scores = lax.dot_general(
            heads.astype(BF16), keys[cache, cols], NT, preferred_element_type=F32
        )
        scores = scores + bias
        own = jnp.sum(heads * key_tall, axis=1, keepdims=True)
        peak = jnp.maximum(jnp.max(scores, axis=1, keepdims=True), own)
        raw = jnp.exp2((scores - peak) * scale)
        raw_own = jnp.exp2((own - peak) * scale)
        share = 1.0 / (jnp.sum(raw, axis=1, keepdims=True) + raw_own)
        result = (dot(raw.astype(BF16), values[cache, cols]) + raw_own * value_tall) * share
        for g in range(GROUP):
            attended[mine, first + g * HEAD_DIM : first + (g + 1) * HEAD_DIM] = result[
                g * SUB : (g + 1) * SUB, :
            ]


def combine_weights(table, ids, gates):
    ids = tile_lanes(ids)
    gates = tile_lanes(gates)
    expert = iota((EXPERTS, EXPERTS), 0)
    gate = jnp.zeros((EXPERTS, EXPERTS), F32)
    for k in range(TOP):
        gate = jnp.where(ids[k : k + 1, :] == expert, gates[k : k + 1, :], gate)
    gate = jnp.transpose(gate)[:ROWS_DEV]
    high = gate.astype(BF16)
    low = (gate - high.astype(F32)).astype(BF16)
    table = jnp.transpose(table)[:ROWS_DEV].astype(BF16)
    spread = (iota((EXPERTS, LINES), 1) // SLOTS == iota((EXPERTS, LINES), 0)).astype(BF16)
    wanted = (iota((ROWS_DEV, LINES), 1) % SLOTS + 1).astype(F32)
    live = dot(table, spread) == wanted
    return [jnp.where(live, dot(part, spread), 0.0).astype(BF16) for part in (high, low)]


def dispatch_weights(table):
    spread = (iota((LINES, EXPERTS), 0) // SLOTS == iota((LINES, EXPERTS), 1)).astype(BF16)
    wanted = (iota((LINES, EXPERTS), 0) % SLOTS + 1).astype(F32)
    full = jnp.where(dot(spread, table.astype(BF16)) == wanted, 1.0, 0.0)
    return full[:, :ROWS_DEV].astype(BF16)


def attention_kernel(
    lengths_hbm,
    ids_hbm,
    gates_hbm,
    gain_hbm,
    hidden_hbm,
    queries_hbm,
    new_keys_hbm,
    new_values_hbm,
    keys_hbm,
    values_hbm,
    o_hbm,
    gate_hbm,
    up_hbm,
    after_ref,
    outgoing_ref,
    mixing_ref,
    gate_ref,
    up_ref,
    lengths,
    ids,
    gates,
    gain,
    hidden,
    queries,
    new_keys,
    new_values,
    keys,
    values,
    o_weight,
    attended,
    dispatch,
    small_sem,
    key_sem,
    value_sem,
    o_sem,
    weight_sem,
):
    pairs = (
        (ids_hbm, ids),
        (gates_hbm, gates),
        (queries_hbm, queries),
        (new_keys_hbm, new_keys),
        (new_values_hbm, new_values),
        (lengths_hbm, lengths),
        (hidden_hbm, hidden),
        (gain_hbm, gain),
    )
    small = [
        pltpu.make_async_copy(source, target, small_sem.at[i])
        for i, (source, target) in enumerate(pairs)
    ]
    for copy in small:
        copy.start()
    key_copies, value_copies, o_copies = [], [], []
    depth = ROWS_DEV * LMAX // HALVES
    for half in range(HALVES):
        part = pl.ds(half * depth, depth)
        key_copies.append(
            pltpu.make_async_copy(keys_hbm.at[part], keys.at[part], key_sem.at[half])
        )
        value_copies.append(
            pltpu.make_async_copy(values_hbm.at[part], values.at[part], value_sem.at[half])
        )
        key_copies[half].start()
        value_copies[half].start()
    for c in range(O_CHUNKS):
        part = pl.ds(c * O_DEPTH, O_DEPTH)
        o_copies.append(pltpu.make_async_copy(o_hbm.at[part], o_weight.at[part], o_sem.at[c]))
    weight_copies = []
    for i, (source, target) in enumerate(
        ((gate_hbm, gate_ref), (up_hbm, up_ref))
    ):
        depth = source.shape[0] // WEIGHT_PARTS
        for c in range(WEIGHT_PARTS):
            part = pl.ds(c * depth, depth)
            weight_copies.append(
                pltpu.make_async_copy(source.at[part], target.at[part], weight_sem.at[i, c])
            )

    for copy in small[:2]:
        copy.wait()
    table = slot_table(ids[...])
    dispatch[...] = dispatch_weights(table)
    high, low = combine_weights(table, ids[...], gates[...])
    mixing_ref[:ROWS_DEV, :] = high
    mixing_ref[ROWS_DEV:, :] = low

    for copy in o_copies:
        copy.start()
    for copy in small[2:]:
        copy.wait()
    for group in range(GROUPS):
        half, later = divmod(group, GROUPS // HALVES)
        if later == 0:
            key_copies[half].wait()
            value_copies[half].wait()
            for copy in ((), weight_copies)[half]:
                copy.start()
        attend_group(group, lengths, queries, new_keys, new_values, keys, values, attended)

    total = hidden[...].astype(F32)
    for c in range(O_CHUNKS):
        o_copies[c].wait()
        part = slice(c * O_DEPTH, (c + 1) * O_DEPTH)
        total = total + dot(attended[:, part].astype(BF16), o_weight[part, :])
    after = total.astype(BF16)
    after_ref[...] = after
    after = after.astype(F32)
    mean = jnp.mean(after * after, axis=1, keepdims=True)
    normed = (after * lax.rsqrt(mean + 1e-6) * gain[...]).astype(BF16)
    for c in range(0, D, OUT_CHUNK):
        part = dot(dispatch[...], normed[:, c : c + OUT_CHUNK]).astype(BF16)
        outgoing_ref[:, :, c : c + OUT_CHUNK] = part.reshape(EXPERTS, SLOTS, OUT_CHUNK)
    for copy in weight_copies:
        copy.wait()


def attention_part(
    lengths,
    ids,
    gates,
    gain,
    hidden,
    queries,
    new_keys,
    new_values,
    keys,
    values,
    o_weight,
    w_gate,
    w_up,
):
    cache = (ROWS_DEV * LMAX, KV_HEADS * HEAD_DIM)
    return pl.pallas_call(
        attention_kernel,
        out_shape=(
            pltpu.VMEM((ROWS_DEV, D), BF16),
            pltpu.VMEM((EXPERTS, SLOTS, D), BF16),
            pltpu.VMEM((2 * ROWS_DEV, LINES), BF16),
            pltpu.VMEM((D, FF), BF16),
            pltpu.VMEM((D, FF), BF16),
        ),
        in_specs=[HBM] * 13,
        out_specs=(VMEM,) * 5,
        scratch_shapes=[
            pltpu.SMEM((ROWS_DEV,), jnp.int32),
            pltpu.VMEM((TOP, ROWS_DEV), jnp.int32),
            pltpu.VMEM((TOP, ROWS_DEV), F32),
            pltpu.VMEM((1, D), F32),
            pltpu.VMEM((ROWS_DEV, D), BF16),
            pltpu.VMEM((ROWS_DEV, D), BF16),
            pltpu.VMEM((ROWS_DEV, KV_HEADS * HEAD_DIM), BF16),
            pltpu.VMEM((ROWS_DEV, KV_HEADS * HEAD_DIM), BF16),
            pltpu.VMEM(cache, BF16),
            pltpu.VMEM(cache, BF16),
            pltpu.VMEM((D, D), BF16),
            pltpu.VMEM((ROWS_DEV, D), F32),
            pltpu.VMEM((LINES, ROWS_DEV), BF16),
            pltpu.SemaphoreType.DMA((8,)),
            pltpu.SemaphoreType.DMA((HALVES,)),
            pltpu.SemaphoreType.DMA((HALVES,)),
            pltpu.SemaphoreType.DMA((O_CHUNKS,)),
            pltpu.SemaphoreType.DMA((3, WEIGHT_PARTS)),
        ],
        compiler_params=pltpu.CompilerParams(vmem_limit_bytes=53 * MIB),
        cost_estimate=pl.CostEstimate(
            flops=2 * ROWS_DEV * D * D, bytes_accessed=16 * MIB, transcendentals=0
        ),
        name="attend",
    )(
        lengths,
        ids,
        gates,
        gain,
        hidden,
        queries,
        new_keys,
        new_values,
        keys,
        values,
        o_weight,
        w_gate,
        w_up,
    )


def expert_kernel(received_ref, gate_ref, up_ref, down_ref, out_ref, rows, inner):
    lines = LINES // EXPERT_PARTS
    sources = EXPERTS // EXPERT_PARTS
    for p in range(EXPERT_PARTS):
        mine = slice(p * lines, (p + 1) * lines)
        there = slice(p * sources, (p + 1) * sources)
        rows[mine, :] = received_ref[there, :, :].reshape(lines, D)
        for f in range(0, FF, FF_CHUNK):
            gate = dot(rows[mine, :], gate_ref[:, f : f + FF_CHUNK])
            up = dot(rows[mine, :], up_ref[:, f : f + FF_CHUNK])
            inner[mine, f : f + FF_CHUNK] = (gate / (1.0 + jnp.exp(-gate)) * up).astype(BF16)
        for c in range(0, D, OUT_CHUNK):
            part = dot(inner[mine, :], down_ref[:, c : c + OUT_CHUNK]).astype(BF16)
            out_ref[there, :, c : c + OUT_CHUNK] = part.reshape(sources, SLOTS, OUT_CHUNK)


def expert_part(received, w_gate, w_up, w_down):
    return pl.pallas_call(
        expert_kernel,
        out_shape=pltpu.VMEM((EXPERTS, SLOTS, D), BF16),
        in_specs=[VMEM] * 4,
        out_specs=VMEM,
        scratch_shapes=[pltpu.VMEM((LINES, D), BF16), pltpu.VMEM((LINES, FF), BF16)],
        compiler_params=pltpu.CompilerParams(vmem_limit_bytes=32 * MIB),
        cost_estimate=pl.CostEstimate(
            flops=6 * LINES * D * FF, bytes_accessed=12 * MIB, transcendentals=0
        ),
        name="experts",
    )(received, w_gate, w_up, w_down)


def combine_kernel(returned_ref, mixing_ref, after_ref, out_hbm, out, sem):
    copies = []
    for c in range(0, D, OUT_CHUNK):
        cols = slice(c, c + OUT_CHUNK)
        mix = dot(mixing_ref[...], returned_ref[:, :, cols].reshape(LINES, OUT_CHUNK))
        mix = mix[:ROWS_DEV] + mix[ROWS_DEV:]
        out[:, cols] = (after_ref[:, cols].astype(F32) + mix).astype(BF16)
        here = pl.ds(c, OUT_CHUNK)
        copies.append(
            pltpu.make_async_copy(out.at[:, here], out_hbm.at[:, here], sem.at[c // OUT_CHUNK])
        )
        copies[-1].start()
    for copy in copies:
        copy.wait()


def combine(returned, mixing, after):
    return pl.pallas_call(
        combine_kernel,
        out_shape=jax.ShapeDtypeStruct((ROWS_DEV, D), BF16),
        in_specs=[VMEM] * 3,
        out_specs=HBM,
        scratch_shapes=[
            pltpu.VMEM((ROWS_DEV, D), BF16),
            pltpu.SemaphoreType.DMA((D // OUT_CHUNK,)),
        ],
        compiler_params=pltpu.CompilerParams(vmem_limit_bytes=24 * MIB),
        cost_estimate=pl.CostEstimate(
            flops=4 * ROWS_DEV * LINES * D, bytes_accessed=4 * MIB, transcendentals=0
        ),
        name="combine",
    )(returned, mixing, after)


def exchange(array):
    return lax.all_to_all(array, ("sec", "dev"), split_axis=0, concat_axis=0, tiled=True)


def on_device(
    hidden_state,
    queries,
    new_keys,
    new_values,
    cache_keys,
    cache_values,
    lengths,
    o_weight,
    norm_gain,
    expert_ids,
    gate_values,
    w_gate,
    w_up,
    w_down,
):
    after, outgoing, mixing, *weights = attention_part(
        lengths,
        expert_ids.T,
        gate_values.T,
        norm_gain.reshape(1, D),
        hidden_state,
        queries,
        new_keys,
        new_values,
        cache_keys.reshape(-1, KV_HEADS * HEAD_DIM),
        cache_values.reshape(-1, KV_HEADS * HEAD_DIM),
        o_weight,
        w_gate.reshape(D, FF),
        w_up.reshape(D, FF),
    )
    made = expert_part(exchange(outgoing), *weights, w_down.reshape(FF, D))
    return combine(exchange(made), mixing, after)


def solution(mesh):
    split = ("sec", "dev")
    rows = P(split, None)
    stack = P(split, None, None)
    return jax.shard_map(
        on_device,
        mesh=mesh,
        in_specs=(
            rows,
            rows,
            rows,
            rows,
            stack,
            stack,
            P(split),
            P(),
            P(),
            rows,
            rows,
            stack,
            stack,
            stack,
        ),
        out_specs=rows,
        check_vma=False,
    )
```

```python
import math

import jax
import jax.numpy as jnp
from jax import lax
from jax.experimental import pallas as pl
from jax.experimental.pallas import tpu as pltpu
from jax.sharding import PartitionSpec as P

D = 2048
FF = 768
KV_HEADS = 2
HEAD_DIM = 128
GROUP = 8
TOP = 8
MICRO = 16
ROWS_DEV = 32
LMAX = 96
MOST = 2
EXPERTS = 128

SLOTS = MOST * ROWS_DEV // MICRO
LINES = EXPERTS * SLOTS
COPIES = EXPERTS // ROWS_DEV

SUB = 8
GROUPS = ROWS_DEV // SUB
HALVES = 2
O_CHUNKS = 4
O_DEPTH = D // O_CHUNKS
WEIGHT_PARTS = 1
FF_CHUNK = 256

OUT_CHUNK = 2048

MIB = 2**20
F32 = jnp.float32
BF16 = jnp.bfloat16
NT = (((1,), (1,)), ((), ()))
VMEM = pl.BlockSpec(memory_space=pltpu.VMEM)
HBM = pl.BlockSpec(memory_space=pltpu.HBM)


def iota(shape, dim):
    return lax.broadcasted_iota(jnp.int32, shape, dim)


def dot(a, b):
    return jnp.dot(a, b, preferred_element_type=F32)


def tile_lanes(array):
    return jnp.concatenate([array] * COPIES, axis=1)


def slot_table(ids):
    ids = tile_lanes(ids)
    square = (EXPERTS, EXPERTS)
    expert = iota(square, 0)
    named = jnp.zeros(square, F32)
    for k in range(TOP):
        named = jnp.where(ids[k : k + 1, :] == expert, 1.0, named)
    first, second = iota(square, 0), iota(square, 1)
    before = jnp.where((first // MICRO == second // MICRO) & (first < second), 1.0, 0.0)
    earlier = dot(named.astype(BF16), before.astype(BF16))
    micro = (iota(square, 1) % ROWS_DEV) // MICRO
    return named * (earlier + (micro * MOST + 1).astype(F32))


def attend_group(group, lengths, queries, new_keys, new_values, keys, values, attended):
    scale = HEAD_DIM ** (-0.5) * math.log2(math.e)
    mine = pl.ds(group * SUB, SUB)
    query = queries[mine, :].astype(F32)
    own_key = new_keys[mine, :].astype(F32)
    own_value = new_values[mine, :].astype(F32)
    cache = pl.ds(group * SUB * LMAX, SUB * LMAX)
    row = iota((SUB, SUB * LMAX), 0)
    length = jnp.zeros((SUB, SUB * LMAX), jnp.int32)
    for r in range(SUB):
        length = jnp.where(row == r, lengths[group * SUB + r], length)
    place = iota((SUB, SUB * LMAX), 1) - row * LMAX
    bias = jnp.where((place >= 0) & (place < length), 0.0, -jnp.inf)
    bias = jnp.concatenate([bias] * GROUP, axis=0)
    for kv in range(KV_HEADS):
        cols = slice(kv * HEAD_DIM, (kv + 1) * HEAD_DIM)
        first = kv * GROUP * HEAD_DIM
        heads = jnp.concatenate(
            [query[:, first + g * HEAD_DIM : first + (g + 1) * HEAD_DIM] for g in range(GROUP)],
            axis=0,
        )
        key_tall = jnp.concatenate([own_key[:, cols]] * GROUP, axis=0)
        value_tall = jnp.concatenate([own_value[:, cols]] * GROUP, axis=0)
        scores = lax.dot_general(
            heads.astype(BF16), keys[cache, cols], NT, preferred_element_type=F32
        )
        scores = scores + bias
        own = jnp.sum(heads * key_tall, axis=1, keepdims=True)
        peak = jnp.maximum(jnp.max(scores, axis=1, keepdims=True), own)
        raw = jnp.exp2((scores - peak) * scale)
        raw_own = jnp.exp2((own - peak) * scale)
        share = 1.0 / (jnp.sum(raw, axis=1, keepdims=True) + raw_own)
        result = (dot(raw.astype(BF16), values[cache, cols]) + raw_own * value_tall) * share
        for g in range(GROUP):
            attended[mine, first + g * HEAD_DIM : first + (g + 1) * HEAD_DIM] = result[
                g * SUB : (g + 1) * SUB, :
            ]


def combine_weights(table, ids, gates):
    ids = tile_lanes(ids)
    gates = tile_lanes(gates)
    expert = iota((EXPERTS, EXPERTS), 0)
    gate = jnp.zeros((EXPERTS, EXPERTS), F32)
    for k in range(TOP):
        gate = jnp.where(ids[k : k + 1, :] == expert, gates[k : k + 1, :], gate)
    gate = jnp.transpose(gate)[:ROWS_DEV]
    high = gate.astype(BF16)
    low = (gate - high.astype(F32)).astype(BF16)
    table = jnp.transpose(table)[:ROWS_DEV].astype(BF16)
    spread = (iota((EXPERTS, LINES), 1) // SLOTS == iota((EXPERTS, LINES), 0)).astype(BF16)
    wanted = (iota((ROWS_DEV, LINES), 1) % SLOTS + 1).astype(F32)
    live = dot(table, spread) == wanted
    return [jnp.where(live, dot(part, spread), 0.0).astype(BF16) for part in (high, low)]


def dispatch_weights(table):
    spread = (iota((LINES, EXPERTS), 0) // SLOTS == iota((LINES, EXPERTS), 1)).astype(BF16)
    wanted = (iota((LINES, EXPERTS), 0) % SLOTS + 1).astype(F32)
    full = jnp.where(dot(spread, table.astype(BF16)) == wanted, 1.0, 0.0)
    return full[:, :ROWS_DEV].astype(BF16)


def attention_kernel(
    lengths_hbm,
    ids_hbm,
    gates_hbm,
    gain_hbm,
    hidden_hbm,
    queries_hbm,
    new_keys_hbm,
    new_values_hbm,
    keys_hbm,
    values_hbm,
    o_hbm,
    gate_hbm,
    up_hbm,
    after_ref,
    outgoing_ref,
    mixing_ref,
    gate_ref,
    up_ref,
    lengths,
    ids,
    gates,
    gain,
    hidden,
    queries,
    new_keys,
    new_values,
    keys,
    values,
    o_weight,
    attended,
    dispatch,
    small_sem,
    key_sem,
    value_sem,
    o_sem,
    weight_sem,
):
    pairs = (
        (ids_hbm, ids),
        (gates_hbm, gates),
        (queries_hbm, queries),
        (new_keys_hbm, new_keys),
        (new_values_hbm, new_values),
        (lengths_hbm, lengths),
        (hidden_hbm, hidden),
        (gain_hbm, gain),
    )
    small = [
        pltpu.make_async_copy(source, target, small_sem.at[i])
        for i, (source, target) in enumerate(pairs)
    ]
    for copy in small:
        copy.start()
    key_copies, value_copies, o_copies = [], [], []
    depth = ROWS_DEV * LMAX // HALVES
    for half in range(HALVES):
        part = pl.ds(half * depth, depth)
        key_copies.append(
            pltpu.make_async_copy(keys_hbm.at[part], keys.at[part], key_sem.at[half])
        )
        value_copies.append(
            pltpu.make_async_copy(values_hbm.at[part], values.at[part], value_sem.at[half])
        )
        key_copies[half].start()
        value_copies[half].start()
    for c in range(O_CHUNKS):
        part = pl.ds(c * O_DEPTH, O_DEPTH)
        o_copies.append(pltpu.make_async_copy(o_hbm.at[part], o_weight.at[part], o_sem.at[c]))
    weight_copies = []
    for i, (source, target) in enumerate(
        ((gate_hbm, gate_ref), (up_hbm, up_ref))
    ):
        depth = source.shape[0] // WEIGHT_PARTS
        for c in range(WEIGHT_PARTS):
            part = pl.ds(c * depth, depth)
            weight_copies.append(
                pltpu.make_async_copy(source.at[part], target.at[part], weight_sem.at[i, c])
            )

    for copy in small[:2]:
        copy.wait()
    table = slot_table(ids[...])
    dispatch[...] = dispatch_weights(table)
    high, low = combine_weights(table, ids[...], gates[...])
    mixing_ref[:ROWS_DEV, :] = high
    mixing_ref[ROWS_DEV:, :] = low

    for copy in o_copies:
        copy.start()
    for copy in small[2:]:
        copy.wait()
    for group in range(GROUPS):
        half, later = divmod(group, GROUPS // HALVES)
        if later == 0:
            key_copies[half].wait()
            value_copies[half].wait()
            for copy in ((), weight_copies)[half]:
                copy.start()
        attend_group(group, lengths, queries, new_keys, new_values, keys, values, attended)

    total = hidden[...].astype(F32)
    for c in range(O_CHUNKS):
        o_copies[c].wait()
        part = slice(c * O_DEPTH, (c + 1) * O_DEPTH)
        total = total + dot(attended[:, part].astype(BF16), o_weight[part, :])
    after = total.astype(BF16)
    after_ref[...] = after
    after = after.astype(F32)
    mean = jnp.mean(after * after, axis=1, keepdims=True)
    normed = (after * lax.rsqrt(mean + 1e-6) * gain[...]).astype(BF16)
    for c in range(0, D, OUT_CHUNK):
        part = dot(dispatch[...], normed[:, c : c + OUT_CHUNK]).astype(BF16)
        outgoing_ref[:, :, c : c + OUT_CHUNK] = part.reshape(EXPERTS, SLOTS, OUT_CHUNK)
    for copy in weight_copies:
        copy.wait()


def attention_part(
    lengths,
    ids,
    gates,
    gain,
    hidden,
    queries,
    new_keys,
    new_values,
    keys,
    values,
    o_weight,
    w_gate,
    w_up,
):
    cache = (ROWS_DEV * LMAX, KV_HEADS * HEAD_DIM)
    return pl.pallas_call(
        attention_kernel,
        out_shape=(
            pltpu.VMEM((ROWS_DEV, D), BF16),
            pltpu.VMEM((EXPERTS, SLOTS, D), BF16),
            pltpu.VMEM((2 * ROWS_DEV, LINES), BF16),
            pltpu.VMEM((D, FF), BF16),
            pltpu.VMEM((D, FF), BF16),
        ),
        in_specs=[HBM] * 13,
        out_specs=(VMEM,) * 5,
        scratch_shapes=[
            pltpu.SMEM((ROWS_DEV,), jnp.int32),
            pltpu.VMEM((TOP, ROWS_DEV), jnp.int32),
            pltpu.VMEM((TOP, ROWS_DEV), F32),
            pltpu.VMEM((1, D), F32),
            pltpu.VMEM((ROWS_DEV, D), BF16),
            pltpu.VMEM((ROWS_DEV, D), BF16),
            pltpu.VMEM((ROWS_DEV, KV_HEADS * HEAD_DIM), BF16),
            pltpu.VMEM((ROWS_DEV, KV_HEADS * HEAD_DIM), BF16),
            pltpu.VMEM(cache, BF16),
            pltpu.VMEM(cache, BF16),
            pltpu.VMEM((D, D), BF16),
            pltpu.VMEM((ROWS_DEV, D), F32),
            pltpu.VMEM((LINES, ROWS_DEV), BF16),
            pltpu.SemaphoreType.DMA((8,)),
            pltpu.SemaphoreType.DMA((HALVES,)),
            pltpu.SemaphoreType.DMA((HALVES,)),
            pltpu.SemaphoreType.DMA((O_CHUNKS,)),
            pltpu.SemaphoreType.DMA((3, WEIGHT_PARTS)),
        ],
        compiler_params=pltpu.CompilerParams(vmem_limit_bytes=53 * MIB),
        cost_estimate=pl.CostEstimate(
            flops=2 * ROWS_DEV * D * D, bytes_accessed=16 * MIB, transcendentals=0
        ),
        name="attend",
    )(
        lengths,
        ids,
        gates,
        gain,
        hidden,
        queries,
        new_keys,
        new_values,
        keys,
        values,
        o_weight,
        w_gate,
        w_up,
    )


def expert_kernel(received_ref, gate_ref, up_ref, down_ref, out_ref, rows, inner):
    rows[...] = received_ref[...].reshape(LINES, D)
    for f in range(0, FF, FF_CHUNK):
        gate = dot(rows[...], gate_ref[:, f : f + FF_CHUNK])
        up = dot(rows[...], up_ref[:, f : f + FF_CHUNK])
        inner[:, f : f + FF_CHUNK] = (gate / (1.0 + jnp.exp(-gate)) * up).astype(BF16)
    for c in range(0, D, OUT_CHUNK):
        part = dot(inner[...], down_ref[:, c : c + OUT_CHUNK]).astype(BF16)
        out_ref[:, :, c : c + OUT_CHUNK] = part.reshape(EXPERTS, SLOTS, OUT_CHUNK)


def expert_part(received, w_gate, w_up, w_down):
    return pl.pallas_call(
        expert_kernel,
        out_shape=pltpu.VMEM((EXPERTS, SLOTS, D), BF16),
        in_specs=[VMEM] * 4,
        out_specs=VMEM,
        scratch_shapes=[pltpu.VMEM((LINES, D), BF16), pltpu.VMEM((LINES, FF), BF16)],
        compiler_params=pltpu.CompilerParams(vmem_limit_bytes=32 * MIB),
        cost_estimate=pl.CostEstimate(
            flops=6 * LINES * D * FF, bytes_accessed=12 * MIB, transcendentals=0
        ),
        name="experts",
    )(received, w_gate, w_up, w_down)


def combine_kernel(returned_ref, mixing_ref, after_ref, out_ref):
    for c in range(0, D, OUT_CHUNK):
        cols = slice(c, c + OUT_CHUNK)
        mix = dot(mixing_ref[...], returned_ref[:, :, cols].reshape(LINES, OUT_CHUNK))
        mix = mix[:ROWS_DEV] + mix[ROWS_DEV:]
        out_ref[:, cols] = (after_ref[:, cols].astype(F32) + mix).astype(BF16)


def combine(returned, mixing, after):
    return pl.pallas_call(
        combine_kernel,
        out_shape=jax.ShapeDtypeStruct((ROWS_DEV, D), BF16),
        in_specs=[VMEM] * 3,
        out_specs=VMEM,
        compiler_params=pltpu.CompilerParams(vmem_limit_bytes=24 * MIB),
        cost_estimate=pl.CostEstimate(
            flops=4 * ROWS_DEV * LINES * D, bytes_accessed=4 * MIB, transcendentals=0
        ),
        name="combine",
    )(returned, mixing, after)


def exchange(array):
    return lax.all_to_all(array, ("sec", "dev"), split_axis=0, concat_axis=0, tiled=True)


def on_device(
    hidden_state,
    queries,
    new_keys,
    new_values,
    cache_keys,
    cache_values,
    lengths,
    o_weight,
    norm_gain,
    expert_ids,
    gate_values,
    w_gate,
    w_up,
    w_down,
):
    after, outgoing, mixing, *weights = attention_part(
        lengths,
        expert_ids.T,
        gate_values.T,
        norm_gain.reshape(1, D),
        hidden_state,
        queries,
        new_keys,
        new_values,
        cache_keys.reshape(-1, KV_HEADS * HEAD_DIM),
        cache_values.reshape(-1, KV_HEADS * HEAD_DIM),
        o_weight,
        w_gate.reshape(D, FF),
        w_up.reshape(D, FF),
    )
    made = expert_part(exchange(outgoing), *weights, w_down.reshape(FF, D))
    return combine(exchange(made), mixing, after)


def solution(mesh):
    split = ("sec", "dev")
    rows = P(split, None)
    stack = P(split, None, None)
    return jax.shard_map(
        on_device,
        mesh=mesh,
        in_specs=(
            rows,
            rows,
            rows,
            rows,
            stack,
            stack,
            P(split),
            P(),
            P(),
            rows,
            rows,
            stack,
            stack,
            stack,
        ),
        out_specs=rows,
        check_vma=False,
    )
```
